32 devices in a mesh: ctx: 8 (over z, y), head: 4 (over x, core).
Axes of the slice: x: 2, y: 2, z: 4, core: 2. Of those that a mesh axis runs over, the one named last changes fastest.
Arguments:
- query: bfloat16 [1024, 2048], P('ctx', 'head'), may hold values from -6 to 6
- keys: bfloat16 [1024, 2048], P('ctx', 'head'), may hold values from -10 to 10
- values: bfloat16 [1024, 2048], P('ctx', 'head'), may hold values from -12 to 12
- log_decay: float32 [1024, 16], P('ctx', 'head'), may hold values from -1 to 0
- norm_gain: float32 [2048], P('head'), may hold values from 0.1 to 1.9
- out_weight: bfloat16 [2048, 6144], P('head'), may hold values from -0.1875 to 0.1875
Outputs:
- mixed: bfloat16 [1024, 6144], P('ctx', 'head')
The draws below stay inside these ranges and needn't reach their ends.
All inputs are finite; a program needn't handle non-finite values.
Results may differ from the reference program's by a relative error of at most 0.014.
Values may be sent and summed in bfloat16 or wider, within the bound.
No kernel may reach another device: no remote copies, remote signals or barrier semaphores. Data moves between devices by JAX's collectives and lax.ppermute only.
A program may use at most 128 MiB of HBM per device.

```python
import jax
import jax.numpy as jnp
from jax import lax

D = 6144
DH = 128
TOK_DEV = 128
HEAD_TOTAL = 16
PROMPT_TOKENS = 1024
N_HEAD = 4


def slab_levels(level_key, lower_end, upper_end):
    block_count = PROMPT_TOKENS // TOK_DEV
    raw_level = jax.random.uniform(level_key, (block_count, HEAD_TOTAL), jnp.float32, lower_end, upper_end)
    spread = jnp.repeat(jnp.exp(raw_level), TOK_DEV, axis=0)
    return jnp.repeat(spread, DH, axis=1)


def draw_keys(key, part):
    key_sequence = jax.random.split(jax.random.fold_in(key, 11), 2)
    entries = jnp.clip(jax.random.normal(key_sequence[0], (PROMPT_TOKENS, HEAD_TOTAL * DH), jnp.float32), -3.5, 3.5)
    return (entries * slab_levels(key_sequence[1], -1.2, 1.0)).astype(jnp.bfloat16)


def draw_values(key, part):
    key_sequence = jax.random.split(jax.random.fold_in(key, 23), 2)
    entries = jnp.clip(jax.random.normal(key_sequence[0], (PROMPT_TOKENS, HEAD_TOTAL * DH), jnp.float32), -3.5, 3.5)
    return (entries * slab_levels(key_sequence[1], -1.5, 1.2)).astype(jnp.bfloat16)


def draw_log_decay(key, part):
    key_sequence = jax.random.split(jax.random.fold_in(key, 5), 6)
    fast_share = 0.5
    is_fast = jax.random.uniform(key_sequence[0], (HEAD_TOTAL,)) < fast_share
    fast_rate = jnp.exp(jax.random.uniform(key_sequence[1], (HEAD_TOTAL,), jnp.float32, jnp.log(1.0 / (2.0 * TOK_DEV + 40.0)), jnp.log(1.0 / 30.0)))
    slow_rate = jnp.exp(jax.random.uniform(key_sequence[2], (HEAD_TOTAL,), jnp.float32, jnp.log(0.05), jnp.log(0.4))) / PROMPT_TOKENS
    base_rate = jnp.where(is_fast, fast_rate, slow_rate)
    block_count = PROMPT_TOKENS // TOK_DEV
    factor = jnp.exp(jax.random.uniform(key_sequence[3], (block_count, HEAD_TOTAL), jnp.float32, jnp.log(0.7), jnp.log(2.8)))
    decay_rate_lookup = jnp.repeat(factor, TOK_DEV, axis=0) * base_rate[None, :]
    spike_positions = jax.random.randint(key_sequence[4], (2, HEAD_TOTAL), 0, PROMPT_TOKENS)
    token_offset = jnp.arange(PROMPT_TOKENS)[:, None]
    spike_present = ((token_offset == spike_positions[0][None, :]) | (token_offset == spike_positions[1][None, :])).astype(jnp.float32)
    spike_penalty = jax.random.uniform(key_sequence[5], (PROMPT_TOKENS, HEAD_TOTAL), jnp.float32, 0.2, 0.4)
    return -(decay_rate_lookup - spike_present * jnp.log(1.0 - spike_penalty))


def raised(values, stream_key, source, target, parts, factor):
    owner, partner = [(jnp.arange(values.shape[dim]) // (values.shape[dim] // parts)).reshape([-1 if axis == dim else 1 for axis in range(values.ndim)]) for dim in (source, target)]
    chosen = jax.random.permutation(stream_key, parts)[partner]
    strong = (owner == chosen) | (owner == (partner + parts // 2) % parts)
    return jnp.where(strong, factor * values, values)


def block_levels(rng, extent, cuts, low, largest):
    factor_of, own = 1.0, jax.random.fold_in(rng, 6)
    for position, blocks in cuts:
        draws = jnp.exp(jax.random.uniform(jax.random.fold_in(own, position), (blocks,), jnp.float32, low / len(cuts), largest / len(cuts)))
        factor_of = factor_of * jnp.repeat(draws, extent[position] // blocks).reshape([-1 if axis == position else 1 for axis in range(len(extent))])
    return factor_of


def gaussian(rng, dims, width, reach, pieces=(), held_as=jnp.bfloat16):
    loudness = block_levels(rng, dims, pieces, -0.22, 0.18) if pieces else 1.0
    drawn = jax.random.normal(rng, dims, jnp.float32) * width * loudness
    return jnp.minimum(jnp.maximum(drawn, -reach), reach).astype(held_as)


def noise_with(key, extent, scale, limit, cuts, heavy, kind=jnp.bfloat16):
    drawn = scale * jax.random.normal(key, extent, jnp.float32)
    if cuts:
        drawn = drawn * block_levels(key, extent, cuts, -0.22, 0.18)
    return jnp.clip(raised(drawn, jax.random.fold_in(key, 3), *heavy), -limit, limit).astype(kind)


def setup_inputs(seed: int = 0) -> dict:
    streams_of = jax.random.split(jax.random.key(seed), 7)
    return {
        "query": gaussian(streams_of[0], (PROMPT_TOKENS, HEAD_TOTAL * DH), 1.0, 6.0, ((0, 8), (1, 4))),
        "keys": draw_keys(jax.random.fold_in(streams_of[6], 71), 0),
        "values": draw_values(jax.random.fold_in(streams_of[6], 71), 0),
        "log_decay": draw_log_decay(jax.random.fold_in(streams_of[6], 71), 0),
        "norm_gain": jnp.clip(1.0 + 0.18 * jax.random.normal(streams_of[4], (HEAD_TOTAL * DH,), jnp.float32), 0.1, 1.9),
        "out_weight": noise_with(streams_of[5], (HEAD_TOTAL * DH, D), (HEAD_TOTAL * DH) ** -0.5, 0.1875, ((0, 4),), (0, 1, 4, 2.0)),
    }


def reference(query, keys, values, log_decay, norm_gain, out_weight):
    head_count = log_decay.shape[1]
    full_width = query.shape[1]
    head_dim = full_width // head_count
    block_count = query.shape[0] // TOK_DEV

    def to_blocks(array):
        return array.reshape(block_count, TOK_DEV, head_count, head_dim).transpose(0, 2, 1, 3)
    query_blocks = to_blocks(query)
    key_blocks = to_blocks(keys)
    value_blocks = to_blocks(values)
    decay_blocks = log_decay.reshape(block_count, TOK_DEV, head_count).transpose(0, 2, 1)
    row_index = lax.broadcasted_iota(jnp.int32, (TOK_DEV, TOK_DEV), 0)
    col_index = lax.broadcasted_iota(jnp.int32, (TOK_DEV, TOK_DEV), 1)
    causal = (row_index >= col_index)[None]

    def step(state, item):
        queries, key_rows, value_rows, decay = item
        cumulative = jnp.cumsum(decay, axis=1)
        differ = jnp.where(causal, cumulative[:, :, None] - cumulative[:, None, :], -1e+30)
        scores = jnp.einsum('hte,hse->hts', queries.astype(jnp.float32), key_rows.astype(jnp.float32))
        block_weights = (jnp.exp(differ) * scores).astype(jnp.bfloat16)
        within = jnp.einsum('hts,hse->hte', block_weights.astype(jnp.float32), value_rows.astype(jnp.float32))
        carried_part = jnp.exp(cumulative)[:, :, None] * jnp.einsum('hte,hef->htf', queries.astype(jnp.float32), state, precision=lax.Precision.HIGHEST)
        tail_decay = jnp.exp(cumulative[:, -1:] - cumulative)
        kv_local = jnp.einsum('hte,htf->hef', key_rows.astype(jnp.float32) * tail_decay[:, :, None], value_rows.astype(jnp.float32), precision=lax.Precision.HIGHEST)
        new_state = jnp.exp(cumulative[:, -1])[:, None, None] * state + kv_local
        return (new_state, within + carried_part)
    start_state = jnp.zeros((head_count, head_dim, head_dim), jnp.float32)
    _, outputs = lax.scan(step, start_state, (query_blocks, key_blocks, value_blocks, decay_blocks))
    attn = outputs.transpose(0, 2, 1, 3).reshape(query.shape[0], full_width)
    mean_square = lax.optimization_barrier(jnp.mean(attn * attn, axis=1))
    normed = (attn * lax.rsqrt(mean_square + 1e-05)[:, None] * norm_gain[None, :]).astype(jnp.bfloat16)
    group_width = full_width // N_HEAD
    summed = jnp.zeros((query.shape[0], out_weight.shape[1]), jnp.float32)
    for group in range(N_HEAD):
        piece = jnp.dot(normed[:, group * group_width:(group + 1) * group_width], out_weight[group * group_width:(group + 1) * group_width], preferred_element_type=jnp.float32)
        summed = summed + lax.optimization_barrier(piece.astype(jnp.bfloat16)).astype(jnp.float32)
    return summed.astype(jnp.bfloat16)
```

```python
import functools

import jax
import jax.numpy as jnp
from jax import lax
from jax.experimental import pallas as pl
from jax.experimental.pallas import tpu as pltpu
from jax.sharding import PartitionSpec as P

F32, BF16 = jnp.float32, jnp.bfloat16
HIGHEST = lax.Precision.HIGHEST
VMEM = pl.BlockSpec(memory_space=pltpu.VMEM)
FAR = pl.BlockSpec(memory_space=pltpu.HBM)
LANES = 128
SUBLANES = 16


def call(body, outs, operands, far=0, out_places=None, scratch=(), cost=1.0):
    held = [pltpu.with_memory_space_constraint(o, pltpu.HBM) for o in operands[:far]]
    return pl.pallas_call(
        body,
        out_shape=outs,
        in_specs=[FAR] * far + [VMEM] * (len(operands) - far),
        out_specs=out_places or [VMEM] * len(outs),
        scratch_shapes=scratch,
        cost_estimate=pl.CostEstimate(flops=int(cost * 1e9), bytes_accessed=int(cost * 1e6), transcendentals=0),
        compiler_params=pltpu.CompilerParams(vmem_limit_bytes=32 << 20),
    )(*held, *operands[far:])


def shape(dims, dtype):
    return jax.ShapeDtypeStruct(dims, dtype)


def padded(rows):
    return -(-rows // SUBLANES) * SUBLANES


def split3(value):
    high = value.astype(BF16)
    rest = value - high.astype(F32)
    mid = rest.astype(BF16)
    return high, mid, (rest - mid.astype(F32)).astype(BF16)


def stacked(value, heads):
    parts = list(split3(value))
    fill = padded(3 * heads) - 3 * heads
    if fill:
        parts.append(jnp.zeros((fill, LANES), BF16))
    return jnp.concatenate([part.astype(F32) for part in parts], axis=0).astype(BF16)


def unstacked(rows, heads):
    rows = rows.astype(F32)
    return rows[:heads] + rows[heads : 2 * heads] + rows[2 * heads : 3 * heads]


def triangle(tokens):
    row = lax.broadcasted_iota(jnp.int32, (tokens, tokens), 0)
    col = lax.broadcasted_iota(jnp.int32, (tokens, tokens), 1)
    return row, col


def column_sums(decay):
    row, col = triangle(decay.shape[1])
    lower = jnp.where(row >= col, 1.0, 0.0).astype(F32)
    return lax.dot_general(lower, decay, (((1,), (1,)), ((), ())), precision=HIGHEST)


def row_sums(decay):
    row, col = triangle(decay.shape[1])
    upper = jnp.where(row <= col, 1.0, 0.0).astype(F32)
    return jnp.dot(decay, upper, precision=HIGHEST)


def odd(axis, step=0):
    return (lax.axis_index(axis) >> step) % 2 == 1


def fetch(sources, targets, semaphores):
    copies = [
        pltpu.make_async_copy(source, target, semaphores.at[index])
        for index, (source, target) in enumerate(zip(sources, targets))
    ]
    for copy in copies:
        copy.start()
    return copies


def states_kernel(keys_far, values_far, decay_far, message, keys, values, decay, semaphores):
    for copy in fetch((keys_far, values_far, decay_far), (keys, values, decay), semaphores):
        copy.wait()
    heads, tokens = decay.shape
    width = keys.shape[1] // heads
    column = column_sums(decay[...])
    tail = jnp.exp(column[tokens - 1 : tokens, :] - column)
    for head in range(heads):
        own = slice(head * width, (head + 1) * width)
        faded = (keys[:, own].astype(F32) * tail[:, head : head + 1]).astype(BF16)
        state = lax.dot_general(
            faded, values[:, own], (((0,), (0,)), ((), ())), preferred_element_type=F32
        )
        message[own, :] = state.astype(BF16)
    total = jnp.sum(decay[...], axis=1, keepdims=True)
    message[heads * width :, :] = stacked(jnp.broadcast_to(jnp.exp(total), (heads, LANES)), heads)


def weights_kernel(far_count, weight_far, _, *refs):
    *weights, token, semaphores = refs
    columns = weights[0].shape[1]
    me = lax.axis_index("head")
    copies = []
    for index in range(2 * far_count):
        owner = me ^ ((far_count - 1 - index // 2) << 1) ^ (1 - index % 2)
        source = weight_far.at[:, pl.ds(pl.multiple_of(owner * columns, LANES), columns)]
        copies.append(pltpu.make_async_copy(source, weights[index], semaphores.at[index]))
        copies[-1].start()
    token[...] = jnp.zeros_like(token)
    for copy in copies:
        copy.wait()


def within_kernel(query_far, keys_far, values_far, decay_far, _, within, grown, query, keys, values, decay, semaphores):
    for copy in fetch((query_far, keys_far, values_far, decay_far), (query, keys, values, decay), semaphores):
        copy.wait()
    heads, tokens = decay.shape
    width = keys.shape[1] // heads
    column = column_sums(decay[...])
    line = row_sums(decay[...])
    grown[...] = jnp.exp(column)
    row, col = triangle(tokens)
    for head in range(heads):
        own = slice(head * width, (head + 1) * width)
        scores = lax.dot_general(
            query[:, own], keys[:, own], (((1,), (1,)), ((), ())), preferred_element_type=F32
        )
        differ = jnp.where(row >= col, column[:, head : head + 1] - line[head : head + 1, :], -1e30)
        weights = (jnp.exp(differ) * scores).astype(BF16)
        within[:, own] = jnp.dot(weights, values[:, own], preferred_element_type=F32)


def join_kernel(step, heads, *refs):
    first = step == 0
    if first:
        mine, theirs, _, joined, entering, entering_decay = refs
    else:
        mine, theirs, before, before_decay, joined, entering, entering_decay = refs
    later = odd("ctx", step)
    rows = mine.shape[0] - padded(3 * heads)
    width = rows // heads
    my_decay = unstacked(mine[rows:, :], heads)
    their_decay = unstacked(theirs[rows:, :], heads)
    one = jnp.ones_like(my_decay)
    for_theirs = jnp.where(later, my_decay, one)
    for_mine = jnp.where(later, one, their_decay)
    if first:
        for_entering = jnp.where(later, one, 0.0 * one)
        entering_decay[...] = jnp.where(later, their_decay, one)
    else:
        for_entering = jnp.where(later, before_decay[...], 0.0 * one)
        entering_decay[...] = before_decay[...] * jnp.where(later, their_decay, one)
    for head in range(heads):
        own = slice(head * width, (head + 1) * width)
        row = slice(head, head + 1)
        received = theirs[own, :].astype(F32)
        joined[own, :] = (for_theirs[row] * received + for_mine[row] * mine[own, :].astype(F32)).astype(BF16)
        added = for_entering[row] * received
        entering[own, :] = added if first else before[own, :] + added
    joined[rows:, :] = stacked(my_decay * their_decay, heads)


def attend_kernel(step, heads, query, within, grown, before, before_decay, theirs, gain, message):
    later = odd("ctx", step)
    tokens, full = query.shape
    width = full // heads
    scale = jnp.where(later, before_decay[...], 0.0 * before_decay[...])
    squares = jnp.zeros((tokens, 1), F32)
    for head in range(heads):
        own = slice(head * width, (head + 1) * width)
        state = before[own, :] + scale[head : head + 1] * theirs[own, :].astype(F32)
        carried = jnp.dot(query[:, own], state.astype(BF16), preferred_element_type=F32)
        attn = within[:, own] + grown[:, head : head + 1] * carried
        squares = squares + jnp.sum(attn * attn, axis=1, keepdims=True)
        message[:, own] = (attn * gain[:, own]).astype(BF16)
    high, mid, low = split3(squares)
    lane = lax.broadcasted_iota(jnp.int32, (tokens, LANES), 1)
    pieces = jnp.where(lane == 0, high.astype(F32), 0.0)
    pieces = jnp.where(lane == 1, mid.astype(F32), pieces)
    message[:, full:] = jnp.where(lane == 2, low.astype(F32), pieces).astype(BF16)


def squares_row(mine, theirs, full):
    column = jnp.sum(mine[:, full:].astype(F32) + theirs[:, full:].astype(F32), axis=1, keepdims=True)
    row, col = triangle(mine.shape[0])
    return jnp.sum(jnp.where(row == col, column, 0.0), axis=0, keepdims=True)


def product(mine, theirs, my_weight, their_weight, full):
    return jnp.dot(mine[:, :full], my_weight[...], preferred_element_type=F32) + jnp.dot(
        theirs[:, :full], their_weight[...], preferred_element_type=F32
    )


def away_kernel(full, mine, theirs, my_weight, their_weight, *refs):
    *received, message = refs
    tokens = mine.shape[0]
    blocks = my_weight.shape[1] // LANES
    result = product(mine, theirs, my_weight, their_weight, full)
    for block in range(blocks):
        there = slice(block * tokens, (block + 1) * tokens)
        part = result[:, block * LANES : (block + 1) * LANES]
        for other in received:
            part = part + other[there, :].astype(F32)
        message[there, :] = part.astype(BF16)
    total = squares_row(mine, theirs, full)
    for other in received:
        total = total + unstacked(other[blocks * tokens :, :], 1)
    message[blocks * tokens :, :] = stacked(total, 1)


def home_kernel(full, mine, theirs, my_weight, their_weight, result):
    result[...] = product(mine, theirs, my_weight, their_weight, full)


def finish_kernel(full, mine, theirs, partial, *refs):
    *received, out, staged, semaphores = refs
    tokens, columns = partial.shape
    blocks = columns // LANES
    total = squares_row(mine, theirs, full)
    for other in received:
        total = total + unstacked(other[blocks * tokens :, :], 1)
    row, col = triangle(tokens)
    total = jnp.sum(jnp.where(row == col, total, 0.0), axis=1, keepdims=True)
    scale = lax.rsqrt(total / (full * lax.axis_size("head")) + 1e-05)
    count = semaphores.shape[0]
    copies = []
    for chunk in range(count):
        for block in range(chunk * blocks // count, (chunk + 1) * blocks // count):
            own = slice(block * LANES, (block + 1) * LANES)
            summed = partial[:, own]
            for other in received:
                summed = summed + other[block * tokens : (block + 1) * tokens, :].astype(F32)
            staged[:, own] = (summed * scale).astype(BF16)
        whole = slice(chunk * blocks // count * LANES, (chunk + 1) * blocks // count * LANES)
        copies.append(pltpu.make_async_copy(staged.at[:, whole], out.at[:, whole], semaphores.at[chunk]))
        copies[-1].start()
    for copy in copies:
        copy.wait()


def local(query, keys, values, log_decay, norm_gain, out_weight):
    tokens, full = query.shape
    heads = log_decay.shape[1]
    steps = lax.axis_size("ctx").bit_length() - 1
    groups = lax.axis_size("head")
    columns = out_weight.shape[1] // groups
    decay = log_decay.T
    message_shape = shape((full + padded(3 * heads), LANES), BF16)
    dma = pltpu.SemaphoreType.DMA

    def swap(value, axis, bit):
        count = lax.axis_size(axis)
        return lax.ppermute(value, axis, [(i, i ^ bit) for i in range(count)])

    blocks = [pltpu.VMEM(array.shape, array.dtype) for array in (query, keys, values, decay)]
    (message,) = call(
        states_kernel,
        [message_shape],
        (keys, values, decay),
        far=3,
        scratch=[*blocks[1:], dma((3,))],
    )
    theirs = swap(message, "ctx", 1)

    far_count = groups // 2
    *weights, token = call(
        functools.partial(weights_kernel, far_count),
        [shape((full, columns), BF16)] * (2 * far_count) + [shape((8, LANES), F32)],
        (out_weight, message),
        far=1,
        scratch=[dma((2 * far_count,))],
        cost=2.0,
    )
    my_weights, their_weights = {}, {}
    for index in range(0, 2 * far_count, 2):
        far = far_count - 1 - index // 2
        their_weights[far] = swap(weights[index], "head", 1)
        my_weights[far] = weights[index + 1]

    entering = (token,)
    for step in range(steps - 1):
        message, *entering = call(
            functools.partial(join_kernel, step, heads),
            [message_shape, shape((full, LANES), F32), shape((heads, LANES), F32)],
            (message, theirs, *entering),
            cost=30.0 if step == steps - 2 else 0.1,
        )
        theirs = swap(message, "ctx", 2 << step)
        if step == 0:
            within, grown = call(
                within_kernel,
                [shape((tokens, full), F32), shape((tokens, heads), F32)],
                (query, keys, values, decay, message),
                far=4,
                scratch=[*blocks, dma((4,))],
                cost=1.0,
            )
    (mine,) = call(
        functools.partial(attend_kernel, steps - 1, heads),
        [shape((tokens, full + LANES), BF16)],
        (query, within, grown, *entering, theirs, norm_gain[None, :]),
    )
    mate = swap(mine, "head", 1)

    received = [[] for _ in range(far_count)]
    reach = far_count // 2
    while reach:
        for far in range(reach, 2 * reach):
            (away,) = call(
                functools.partial(away_kernel, full),
                [shape((columns // LANES * tokens + SUBLANES, LANES), BF16)],
                (mine, mate, my_weights[far], their_weights[far], *received[far]),
            )
            received[far - reach].append(swap(away, "head", reach << 1))
        reach //= 2
    (partial,) = call(
        functools.partial(home_kernel, full),
        [shape((tokens, columns), F32)],
        (mine, mate, my_weights[0], their_weights[0]),
    )
    (mixed,) = call(
        functools.partial(finish_kernel, full),
        [shape((tokens, columns), BF16)],
        (mine, mate, partial, *received[0]),
        out_places=[FAR],
        scratch=[pltpu.VMEM((tokens, columns), BF16), dma((3,))],
    )
    return mixed


def solution(mesh):
    placed = (
        P("ctx", "head"),
        P("ctx", "head"),
        P("ctx", "head"),
        P("ctx", "head"),
        P("head"),
        P("head", None),
    )
    return jax.shard_map(
        local, mesh=mesh, in_specs=placed, out_specs=P("ctx", "head"), check_vma=False
    )
```

```python
import functools

import jax
import jax.numpy as jnp
from jax import lax
from jax.experimental import pallas as pl
from jax.experimental.pallas import tpu as pltpu
from jax.sharding import PartitionSpec as P

F32, BF16 = jnp.float32, jnp.bfloat16
HIGHEST = lax.Precision.HIGHEST
VMEM = pl.BlockSpec(memory_space=pltpu.VMEM)
FAR = pl.BlockSpec(memory_space=pltpu.HBM)
LANES = 128
SUBLANES = 16
PARTS = 3


def call(body, outs, operands, far=0, out_places=None, scratch=(), cost=1.0):
    held = [pltpu.with_memory_space_constraint(o, pltpu.HBM) for o in operands[:far]]
    return pl.pallas_call(
        body,
        out_shape=outs,
        in_specs=[FAR] * far + [VMEM] * (len(operands) - far),
        out_specs=out_places or [VMEM] * len(outs),
        scratch_shapes=scratch,
        cost_estimate=pl.CostEstimate(flops=int(cost * 1e9), bytes_accessed=int(cost * 1e6), transcendentals=0),
        compiler_params=pltpu.CompilerParams(vmem_limit_bytes=32 << 20),
    )(*held, *operands[far:])


def shape(dims, dtype):
    return jax.ShapeDtypeStruct(dims, dtype)


def padded(rows):
    return -(-rows // SUBLANES) * SUBLANES


def split3(value):
    high = value.astype(BF16)
    rest = value - high.astype(F32)
    mid = rest.astype(BF16)
    return high, mid, (rest - mid.astype(F32)).astype(BF16)


def stacked(value, heads):
    parts = list(split3(value))
    fill = padded(3 * heads) - 3 * heads
    if fill:
        parts.append(jnp.zeros((fill, LANES), BF16))
    return jnp.concatenate([part.astype(F32) for part in parts], axis=0).astype(BF16)


def unstacked(rows, heads):
    rows = rows.astype(F32)
    return rows[:heads] + rows[heads : 2 * heads] + rows[2 * heads : 3 * heads]


def triangle(tokens):
    row = lax.broadcasted_iota(jnp.int32, (tokens, tokens), 0)
    col = lax.broadcasted_iota(jnp.int32, (tokens, tokens), 1)
    return row, col


def column_sums(decay):
    row, col = triangle(decay.shape[1])
    lower = jnp.where(row >= col, 1.0, 0.0).astype(F32)
    return lax.dot_general(lower, decay, (((1,), (1,)), ((), ())), precision=HIGHEST)


def row_sums(decay):
    row, col = triangle(decay.shape[1])
    upper = jnp.where(row <= col, 1.0, 0.0).astype(F32)
    return jnp.dot(decay, upper, precision=HIGHEST)


def odd(axis, step=0):
    return (lax.axis_index(axis) >> step) % 2 == 1


def fetch(sources, targets, semaphores):
    copies = [
        pltpu.make_async_copy(source, target, semaphores.at[index])
        for index, (source, target) in enumerate(zip(sources, targets))
    ]
    for copy in copies:
        copy.start()
    return copies


def states_kernel(keys_far, values_far, decay_far, message, keys, values, decay, semaphores):
    decay_copy, *copies = fetch((decay_far, keys_far, values_far), (decay, keys, values), semaphores)
    decay_copy.wait()
    heads, tokens = decay.shape
    width = keys.shape[1] // heads
    column = column_sums(decay[...])
    for copy in copies:
        copy.wait()
    tail = jnp.exp(column[tokens - 1 : tokens, :] - column)
    for head in range(heads):
        own = slice(head * width, (head + 1) * width)
        faded = (keys[:, own].astype(F32) * tail[:, head : head + 1]).astype(BF16)
        state = lax.dot_general(
            faded, values[:, own], (((0,), (0,)), ((), ())), preferred_element_type=F32
        )
        message[own, :] = state.astype(BF16)
    total = jnp.sum(decay[...], axis=1, keepdims=True)
    message[heads * width :, :] = stacked(jnp.broadcast_to(jnp.exp(total), (heads, LANES)), heads)


def weights_kernel(far_count, weight_far, _, *refs):
    *weights, token, semaphores = refs
    columns = weights[0].shape[1]
    me = lax.axis_index("head")
    copies = []
    for index in range(2 * far_count):
        owner = me ^ ((far_count - 1 - index // 2) << 1) ^ (1 - index % 2)
        source = weight_far.at[:, pl.ds(pl.multiple_of(owner * columns, LANES), columns)]
        copies.append(pltpu.make_async_copy(source, weights[index], semaphores.at[index]))
        copies[-1].start()
    token[...] = jnp.zeros_like(token)
    for copy in copies:
        copy.wait()


def within_kernel(query_far, keys_far, values_far, decay_far, _, within, grown, query, keys, values, decay, semaphores):
    for copy in fetch((query_far, keys_far, values_far, decay_far), (query, keys, values, decay), semaphores):
        copy.wait()
    heads, tokens = decay.shape
    width = keys.shape[1] // heads
    column = column_sums(decay[...])
    line = row_sums(decay[...])
    grown[...] = jnp.exp(column)
    row, col = triangle(tokens)
    for head in range(heads):
        own = slice(head * width, (head + 1) * width)
        scores = lax.dot_general(
            query[:, own], keys[:, own], (((1,), (1,)), ((), ())), preferred_element_type=F32
        )
        differ = jnp.where(row >= col, column[:, head : head + 1] - line[head : head + 1, :], -1e30)
        weights = (jnp.exp(differ) * scores).astype(BF16)
        within[:, own] = jnp.dot(weights, values[:, own], preferred_element_type=F32)


def join_kernel(step, heads, *refs):
    first = step == 0
    if first:
        mine, theirs, _, joined, entering, entering_decay = refs
    else:
        mine, theirs, before, before_decay, joined, entering, entering_decay = refs
    later = odd("ctx", step)
    rows = mine.shape[0] - padded(3 * heads)
    width = rows // heads
    my_decay = unstacked(mine[rows:, :], heads)
    their_decay = unstacked(theirs[rows:, :], heads)
    one = jnp.ones_like(my_decay)
    for_theirs = jnp.where(later, my_decay, one)
    for_mine = jnp.where(later, one, their_decay)
    if first:
        for_entering = jnp.where(later, one, 0.0 * one)
        entering_decay[...] = jnp.where(later, their_decay, one)
    else:
        for_entering = jnp.where(later, before_decay[...], 0.0 * one)
        entering_decay[...] = before_decay[...] * jnp.where(later, their_decay, one)
    for head in range(heads):
        own = slice(head * width, (head + 1) * width)
        row = slice(head, head + 1)
        received = theirs[own, :].astype(F32)
        joined[own, :] = (for_theirs[row] * received + for_mine[row] * mine[own, :].astype(F32)).astype(BF16)
        added = for_entering[row] * received
        entering[own, :] = added if first else before[own, :] + added
    if joined.shape[0] > rows:
        joined[rows:, :] = stacked(my_decay * their_decay, heads)


def attend_kernel(step, heads, query, within, grown, before, before_decay, theirs, gain, message):
    later = odd("ctx", step)
    tokens, full = query.shape
    width = full // heads
    scale = jnp.where(later, before_decay[...], 0.0 * before_decay[...])
    squares = jnp.zeros((tokens, 1), F32)
    for head in range(heads):
        own = slice(head * width, (head + 1) * width)
        state = before[own, :] + scale[head : head + 1] * theirs[own, :].astype(F32)
        carried = jnp.dot(query[:, own], state.astype(BF16), preferred_element_type=F32)
        attn = within[:, own] + grown[:, head : head + 1] * carried
        squares = squares + jnp.sum(attn * attn, axis=1, keepdims=True)
        message[:, own] = (attn * gain[:, own]).astype(BF16)
    high, mid, low = split3(squares)
    lane = lax.broadcasted_iota(jnp.int32, (tokens, LANES), 1)
    pieces = jnp.where(lane == 0, high.astype(F32), 0.0)
    pieces = jnp.where(lane == 1, mid.astype(F32), pieces)
    message[:, full:] = jnp.where(lane == 2, low.astype(F32), pieces).astype(BF16)


def squares_row(mine, theirs, full):
    column = jnp.sum(mine[:, full:].astype(F32) + theirs[:, full:].astype(F32), axis=1, keepdims=True)
    row, col = triangle(mine.shape[0])
    return jnp.sum(jnp.where(row == col, column, 0.0), axis=0, keepdims=True)


def ahead_kernel(full, mine, weight, result):
    result[...] = jnp.dot(mine[:, :full], weight[...], preferred_element_type=F32)


def away_kernel(full, first_block, partial, mine, theirs, their_weight, *refs):
    *received, message = refs
    tokens = mine.shape[0]
    blocks = message.shape[0] // tokens
    columns = slice(first_block * LANES, (first_block + blocks) * LANES)
    result = partial[:, columns] + jnp.dot(theirs[:, :full], their_weight[:, columns], preferred_element_type=F32)
    for block in range(blocks):
        there = slice(block * tokens, (block + 1) * tokens)
        part = result[:, block * LANES : (block + 1) * LANES]
        for other in received:
            part = part + other[there, :].astype(F32)
        message[there, :] = part.astype(BF16)
    if first_block == 0:
        total = squares_row(mine, theirs, full)
        for other in received:
            total = total + unstacked(other[blocks * tokens :, :], 1)
        message[blocks * tokens :, :] = stacked(total, 1)


def home_kernel(full, mine, theirs, my_weight, their_weight, result):
    result[...] = jnp.dot(mine[:, :full], my_weight[...], preferred_element_type=F32) + jnp.dot(
        theirs[:, :full], their_weight[...], preferred_element_type=F32
    )


def scaled(partial, first_block, received, scale, out):
    tokens, columns = out.shape
    for block in range(columns // LANES):
        summed = partial[:, (first_block + block) * LANES : (first_block + block + 1) * LANES]
        for other in received:
            summed = summed + other[block * tokens : (block + 1) * tokens, :].astype(F32)
        out[:, block * LANES : (block + 1) * LANES] = (summed * scale).astype(BF16)


def first_kernel(full, mine, theirs, partial, *refs):
    *received, scale, out = refs
    tokens, columns = out.shape
    total = squares_row(mine, theirs, full)
    for other in received:
        total = total + unstacked(other[columns // LANES * tokens :, :], 1)
    row, col = triangle(tokens)
    total = jnp.sum(jnp.where(row == col, total, 0.0), axis=1, keepdims=True)
    factor = lax.rsqrt(total / (full * lax.axis_size("head")) + 1e-05)
    scale[...] = factor
    scaled(partial, 0, received, factor, out)


def middle_kernel(first_block, partial, scale, *refs):
    *received, out = refs
    scaled(partial, first_block, received, scale[...], out)


def last_kernel(first_block, done_count, partial, scale, *refs):
    done, received = refs[:done_count], refs[done_count:-3]
    out, staged, semaphores = refs[-3:]
    copies = []

    def write(source, column):
        there = out.at[:, column : column + source.shape[1]]
        copies.append(pltpu.make_async_copy(source, there, semaphores.at[len(copies)]))
        copies[-1].start()

    column = 0
    for part in done:
        write(part, column)
        column += part.shape[1]
    scaled(partial, first_block, received, scale[...], staged)
    write(staged, column)
    for copy in copies:
        copy.wait()


def local(query, keys, values, log_decay, norm_gain, out_weight):
    tokens, full = query.shape
    heads = log_decay.shape[1]
    steps = lax.axis_size("ctx").bit_length() - 1
    groups = lax.axis_size("head")
    columns = out_weight.shape[1] // groups
    decay = log_decay.T
    message_shape = shape((full + padded(3 * heads), LANES), BF16)
    dma = pltpu.SemaphoreType.DMA

    def swap(value, axis, bit):
        count = lax.axis_size(axis)
        return lax.ppermute(value, axis, [(i, i ^ bit) for i in range(count)])

    blocks = [pltpu.VMEM(array.shape, array.dtype) for array in (query, keys, values, decay)]
    (message,) = call(
        states_kernel,
        [message_shape],
        (keys, values, decay),
        far=3,
        scratch=[*blocks[1:], dma((3,))],
    )
    theirs = swap(message, "ctx", 1)

    far_count = groups // 2
    *weights, token = call(
        functools.partial(weights_kernel, far_count),
        [shape((full, columns), BF16)] * (2 * far_count) + [shape((8, LANES), F32)],
        (out_weight, message),
        far=1,
        scratch=[dma((2 * far_count,))],
        cost=2.0,
    )
    my_weights, their_weights = {}, {}
    for index in range(0, 2 * far_count, 2):
        far = far_count - 1 - index // 2
        their_weights[far] = swap(weights[index], "head", 1)
        my_weights[far] = weights[index + 1]

    entering = (token,)
    for step in range(steps - 1):
        message, *entering = call(
            functools.partial(join_kernel, step, heads),
            [
                message_shape if step < steps - 2 else shape((full, LANES), BF16),
                shape((full, LANES), F32),
                shape((heads, LANES), F32),
            ],
            (message, theirs, *entering),
            cost=30.0 if step == steps - 2 else 0.1,
        )
        theirs = swap(message, "ctx", 2 << step)
        if step == 0:
            within, grown = call(
                within_kernel,
                [shape((tokens, full), F32), shape((tokens, heads), F32)],
                (query, keys, values, decay, message),
                far=4,
                scratch=[*blocks, dma((4,))],
                cost=1.0,
            )
    (mine,) = call(
        functools.partial(attend_kernel, steps - 1, heads),
        [shape((tokens, full + LANES), BF16)],
        (query, within, grown, *entering, theirs, norm_gain[None, :]),
    )
    mate = swap(mine, "head", 1)
    ahead = {}
    for far in range(1, far_count):
        (ahead[far],) = call(
            functools.partial(ahead_kernel, full),
            [shape((tokens, columns), F32)],
            (mine, my_weights[far]),
            cost=0.4,
        )

    blocks_out = columns // LANES
    cuts = [0, blocks_out // 4, blocks_out - blocks_out // 6, blocks_out]
    received = [[[] for _ in range(PARTS)] for _ in range(far_count)]
    reach = far_count // 2
    while reach:
        for far in range(reach, 2 * reach):
            for part, (first, end) in enumerate(zip(cuts[:-1], cuts[1:])):
                (away,) = call(
                    functools.partial(away_kernel, full, first),
                    [shape(((end - first) * tokens + (SUBLANES if first == 0 else 0), LANES), BF16)],
                    (ahead[far], mine, mate, their_weights[far], *received[far][part]),
                    cost=0.2,
                )
                received[far - reach][part].append(swap(away, "head", reach << 1))
        reach //= 2
    (partial,) = call(
        functools.partial(home_kernel, full),
        [shape((tokens, columns), F32)],
        (mine, mate, my_weights[0], their_weights[0]),
        cost=0.6,
    )
    widths = [(end - first) * LANES for first, end in zip(cuts[:-1], cuts[1:])]
    scale, part_done = call(
        functools.partial(first_kernel, full),
        [shape((tokens, 1), F32), shape((tokens, widths[0]), BF16)],
        (mine, mate, partial, *received[0][0]),
        cost=0.3,
    )
    done = [part_done]
    for part in range(1, PARTS - 1):
        done += call(
            functools.partial(middle_kernel, cuts[part]),
            [shape((tokens, widths[part]), BF16)],
            (partial, scale, *received[0][part]),
            cost=0.2,
        )
    (mixed,) = call(
        functools.partial(last_kernel, cuts[PARTS - 1], len(done)),
        [shape((tokens, columns), BF16)],
        (partial, scale, *done, *received[0][PARTS - 1]),
        out_places=[FAR],
        scratch=[pltpu.VMEM((tokens, widths[-1]), BF16), dma((PARTS,))],
    )
    return mixed


def solution(mesh):
    placed = (
        P("ctx", "head"),
        P("ctx", "head"),
        P("ctx", "head"),
        P("ctx", "head"),
        P("head"),
        P("head", None),
    )
    return jax.shard_map(
        local, mesh=mesh, in_specs=placed, out_specs=P("ctx", "head"), check_vma=False
    )
```

```python
import functools

import jax
import jax.numpy as jnp
from jax import lax
from jax.experimental import pallas as pl
from jax.experimental.pallas import tpu as pltpu
from jax.sharding import PartitionSpec as P

F32, BF16 = jnp.float32, jnp.bfloat16
HIGHEST = lax.Precision.HIGHEST
VMEM = pl.BlockSpec(memory_space=pltpu.VMEM)
FAR = pl.BlockSpec(memory_space=pltpu.HBM)
LANES = 128
SUBLANES = 16
PARTS = 3


def call(body, outs, operands, far=0, out_places=None, scratch=(), cost=1.0):
    held = [pltpu.with_memory_space_constraint(o, pltpu.HBM) for o in operands[:far]]
    return pl.pallas_call(
        body,
        out_shape=outs,
        in_specs=[FAR] * far + [VMEM] * (len(operands) - far),
        out_specs=out_places or [VMEM] * len(outs),
        scratch_shapes=scratch,
        cost_estimate=pl.CostEstimate(flops=int(cost * 1e9), bytes_accessed=int(cost * 1e6), transcendentals=0),
        compiler_params=pltpu.CompilerParams(vmem_limit_bytes=32 << 20),
    )(*held, *operands[far:])


def shape(dims, dtype):
    return jax.ShapeDtypeStruct(dims, dtype)


def padded(rows):
    return -(-rows // SUBLANES) * SUBLANES


def split3(value):
    high = value.astype(BF16)
    rest = value - high.astype(F32)
    mid = rest.astype(BF16)
    return high, mid, (rest - mid.astype(F32)).astype(BF16)


def stacked(value, heads):
    parts = list(split3(value))
    fill = padded(3 * heads) - 3 * heads
    if fill:
        parts.append(jnp.zeros((fill, LANES), BF16))
    return jnp.concatenate([part.astype(F32) for part in parts], axis=0).astype(BF16)


def unstacked(rows, heads):
    rows = rows.astype(F32)
    return rows[:heads] + rows[heads : 2 * heads] + rows[2 * heads : 3 * heads]


def triangle(tokens):
    row = lax.broadcasted_iota(jnp.int32, (tokens, tokens), 0)
    col = lax.broadcasted_iota(jnp.int32, (tokens, tokens), 1)
    return row, col


def column_sums(decay):
    row, col = triangle(decay.shape[1])
    lower = jnp.where(row >= col, 1.0, 0.0).astype(F32)
    return lax.dot_general(lower, decay, (((1,), (1,)), ((), ())), precision=HIGHEST)


def row_sums(decay):
    row, col = triangle(decay.shape[1])
    upper = jnp.where(row <= col, 1.0, 0.0).astype(F32)
    return jnp.dot(decay, upper, precision=HIGHEST)


def odd(axis, step=0):
    return (lax.axis_index(axis) >> step) % 2 == 1


def fetch(sources, targets, semaphores):
    copies = [
        pltpu.make_async_copy(source, target, semaphores.at[index])
        for index, (source, target) in enumerate(zip(sources, targets))
    ]
    for copy in copies:
        copy.start()
    return copies


def states_kernel(keys_far, values_far, decay_far, message, keys, values, decay, tails, semaphores):
    decay_copy, *copies = fetch((decay_far, keys_far, values_far), (decay, keys, values), semaphores)
    decay_copy.wait()
    heads, tokens = decay.shape
    width = keys.shape[1] // heads
    column = column_sums(decay[...])
    tail = jnp.exp(column[tokens - 1 : tokens, :] - column)
    for head in range(heads):
        tails[:, head * width : (head + 1) * width] = jnp.broadcast_to(tail[:, head : head + 1], (tokens, width))
    total = jnp.sum(decay[...], axis=1, keepdims=True)
    message[heads * width :, :] = stacked(jnp.broadcast_to(jnp.exp(total), (heads, LANES)), heads)
    for copy in copies:
        copy.wait()
    for head in range(heads):
        own = slice(head * width, (head + 1) * width)
        faded = (keys[:, own].astype(F32) * tails[:, own]).astype(BF16)
        state = lax.dot_general(
            faded, values[:, own], (((0,), (0,)), ((), ())), preferred_element_type=F32
        )
        message[own, :] = state.astype(BF16)


def weights_kernel(far_count, weight_far, _, *refs):
    *weights, token, semaphores = refs
    columns = weights[0].shape[1]
    me = lax.axis_index("head")
    copies = []
    for index in range(2 * far_count):
        owner = me ^ ((far_count - 1 - index // 2) << 1) ^ (1 - index % 2)
        source = weight_far.at[:, pl.ds(pl.multiple_of(owner * columns, LANES), columns)]
        copies.append(pltpu.make_async_copy(source, weights[index], semaphores.at[index]))
        copies[-1].start()
    token[...] = jnp.zeros_like(token)
    for copy in copies:
        copy.wait()


def within_kernel(step, query_far, keys_far, values_far, decay_far, before, before_decay, *refs):
    within, factor, query, keys, values, decay, semaphores = refs
    for copy in fetch((query_far, keys_far, values_far, decay_far), (query, keys, values, decay), semaphores):
        copy.wait()
    heads, tokens = decay.shape
    width = keys.shape[1] // heads
    column = column_sums(decay[...])
    line = row_sums(decay[...])
    grown = jnp.exp(column)
    scale = jnp.where(odd("ctx", step), before_decay[...], 0.0 * before_decay[...])
    row, col = triangle(tokens)
    for head in range(heads):
        own = slice(head * width, (head + 1) * width)
        scores = lax.dot_general(
            query[:, own], keys[:, own], (((1,), (1,)), ((), ())), preferred_element_type=F32
        )
        differ = jnp.where(row >= col, column[:, head : head + 1] - line[head : head + 1, :], -1e30)
        weights = (jnp.exp(differ) * scores).astype(BF16)
        carried = jnp.dot(query[:, own], before[own, :].astype(BF16), preferred_element_type=F32)
        spread = jnp.broadcast_to(grown[:, head : head + 1], (tokens, width))
        within[:, own] = jnp.dot(weights, values[:, own], preferred_element_type=F32) + spread * carried
        factor[:, own] = spread * scale[head : head + 1]


def join_kernel(step, heads, *refs):
    first = step == 0
    if first:
        mine, theirs, _, joined, entering, entering_decay = refs
    else:
        mine, theirs, before, before_decay, joined, entering, entering_decay = refs
    later = odd("ctx", step)
    rows = mine.shape[0] - padded(3 * heads)
    width = rows // heads
    my_decay = unstacked(mine[rows:, :], heads)
    their_decay = unstacked(theirs[rows:, :], heads)
    one = jnp.ones_like(my_decay)
    for_theirs = jnp.where(later, my_decay, one)
    for_mine = jnp.where(later, one, their_decay)
    if first:
        for_entering = jnp.where(later, one, 0.0 * one)
        entering_decay[...] = jnp.where(later, their_decay, one)
    else:
        for_entering = jnp.where(later, before_decay[...], 0.0 * one)
        entering_decay[...] = before_decay[...] * jnp.where(later, their_decay, one)
    for head in range(heads):
        own = slice(head * width, (head + 1) * width)
        row = slice(head, head + 1)
        received = theirs[own, :].astype(F32)
        joined[own, :] = (for_theirs[row] * received + for_mine[row] * mine[own, :].astype(F32)).astype(BF16)
        added = for_entering[row] * received
        entering[own, :] = added if first else before[own, :] + added
    if joined.shape[0] > rows:
        joined[rows:, :] = stacked(my_decay * their_decay, heads)


def attend_kernel(heads, query, within, factor, theirs, gain, message):
    tokens, full = query.shape
    width = full // heads
    squares = jnp.zeros((tokens, width), F32)
    for head in range(heads):
        own = slice(head * width, (head + 1) * width)
        carried = jnp.dot(query[:, own], theirs[own, :], preferred_element_type=F32)
        attn = within[:, own] + factor[:, own] * carried
        squares = squares + attn * attn
        message[:, own] = (attn * gain[:, own]).astype(BF16)
    squares = jnp.sum(squares, axis=1, keepdims=True)
    high, mid, low = split3(squares)
    lane = lax.broadcasted_iota(jnp.int32, (tokens, LANES), 1)
    pieces = jnp.where(lane == 0, high.astype(F32), 0.0)
    pieces = jnp.where(lane == 1, mid.astype(F32), pieces)
    message[:, full:] = jnp.where(lane == 2, low.astype(F32), pieces).astype(BF16)


def squares_row(mine, theirs, full):
    column = jnp.sum(mine[:, full:].astype(F32) + theirs[:, full:].astype(F32), axis=1, keepdims=True)
    row, col = triangle(mine.shape[0])
    return jnp.sum(jnp.where(row == col, column, 0.0), axis=0, keepdims=True)


def ahead_kernel(full, mine, weight, result):
    result[...] = jnp.dot(mine[:, :full], weight[...], preferred_element_type=F32)


def away_kernel(full, first_block, leading, partial, mine, theirs, their_weight, *refs):
    *received, message = refs
    tokens = mine.shape[0]
    blocks = message.shape[0] // tokens
    columns = slice(first_block * LANES, (first_block + blocks) * LANES)
    result = partial[:, columns] + jnp.dot(theirs[:, :full], their_weight[:, columns], preferred_element_type=F32)
    for block in range(blocks):
        there = slice(block * tokens, (block + 1) * tokens)
        part = result[:, block * LANES : (block + 1) * LANES]
        for other in received:
            part = part + other[there, :].astype(F32)
        message[there, :] = part.astype(BF16)
    if leading:
        total = squares_row(mine, theirs, full)
        for other in received:
            total = total + unstacked(other[blocks * tokens :, :], 1)
        message[blocks * tokens :, :] = stacked(total, 1)


def home_kernel(full, mine, theirs, my_weight, their_weight, result):
    result[...] = jnp.dot(mine[:, :full], my_weight[...], preferred_element_type=F32) + jnp.dot(
        theirs[:, :full], their_weight[...], preferred_element_type=F32
    )


def scaled(partial, first_block, received, scale, out):
    tokens, columns = out.shape
    for block in range(columns // LANES):
        summed = partial[:, (first_block + block) * LANES : (first_block + block + 1) * LANES]
        for other in received:
            summed = summed + other[block * tokens : (block + 1) * tokens, :].astype(F32)
        out[:, block * LANES : (block + 1) * LANES] = (summed * scale).astype(BF16)


def middle_kernel(full, cuts, count, mine, theirs, partial, *refs):
    received, (scale, *outs) = refs[: len(cuts) * count], refs[len(cuts) * count :]
    groups = [received[part * count : (part + 1) * count] for part in range(len(cuts))]
    total = squares_row(mine, theirs, full)
    for other in groups[-1]:
        total = total + unstacked(other[other.shape[0] - SUBLANES :, :], 1)
    row, col = triangle(mine.shape[0])
    total = jnp.sum(jnp.where(row == col, total, 0.0), axis=1, keepdims=True)
    factor = lax.rsqrt(total / (full * lax.axis_size("head")) + 1e-05)
    scale[...] = factor
    for first_block, group, out in zip(cuts, groups, outs):
        scaled(partial, first_block, group, factor, out)


def last_kernel(first_block, done_count, partial, scale, *refs):
    done, received = refs[:done_count], refs[done_count:-3]
    out, staged, semaphores = refs[-3:]
    copies = []

    def write(source, column):
        there = out.at[:, column : column + source.shape[1]]
        copies.append(pltpu.make_async_copy(source, there, semaphores.at[len(copies)]))
        copies[-1].start()

    column = 0
    for part in done:
        write(part, column)
        column += part.shape[1]
    scaled(partial, first_block, received, scale[...], staged)
    write(staged, column)
    for copy in copies:
        copy.wait()


def local(query, keys, values, log_decay, norm_gain, out_weight):
    tokens, full = query.shape
    heads = log_decay.shape[1]
    steps = lax.axis_size("ctx").bit_length() - 1
    groups = lax.axis_size("head")
    columns = out_weight.shape[1] // groups
    decay = log_decay.T
    message_shape = shape((full + padded(3 * heads), LANES), BF16)
    dma = pltpu.SemaphoreType.DMA

    def swap(value, axis, bit):
        count = lax.axis_size(axis)
        return lax.ppermute(value, axis, [(i, i ^ bit) for i in range(count)])

    blocks = [pltpu.VMEM(array.shape, array.dtype) for array in (query, keys, values, decay)]
    (message,) = call(
        states_kernel,
        [message_shape],
        (keys, values, decay),
        far=3,
        scratch=[*blocks[1:], pltpu.VMEM((tokens, full), F32), dma((3,))],
    )
    theirs = swap(message, "ctx", 1)

    far_count = groups // 2
    *weights, token = call(
        functools.partial(weights_kernel, far_count),
        [shape((full, columns), BF16)] * (2 * far_count) + [shape((8, LANES), F32)],
        (out_weight, message),
        far=1,
        scratch=[dma((2 * far_count,))],
        cost=2.0,
    )
    my_weights, their_weights = {}, {}
    for index in range(0, 2 * far_count, 2):
        far = far_count - 1 - index // 2
        their_weights[far] = swap(weights[index], "head", 1)
        my_weights[far] = weights[index + 1]

    entering = (token,)
    for step in range(steps - 1):
        message, *entering = call(
            functools.partial(join_kernel, step, heads),
            [
                message_shape if step < steps - 2 else shape((full, LANES), BF16),
                shape((full, LANES), F32),
                shape((heads, LANES), F32),
            ],
            (message, theirs, *entering),
            cost=30.0 if step == steps - 2 else 0.1,
        )
        theirs = swap(message, "ctx", 2 << step)
    within, factor = call(
        functools.partial(within_kernel, steps - 1),
        [shape((tokens, full), F32)] * 2,
        (query, keys, values, decay, *entering),
        far=4,
        scratch=[*blocks, dma((4,))],
        cost=1.0,
    )
    (mine,) = call(
        functools.partial(attend_kernel, heads),
        [shape((tokens, full + LANES), BF16)],
        (query, within, factor, theirs, norm_gain[None, :]),
    )
    mate = swap(mine, "head", 1)
    ahead = {}
    for far in range(1, far_count):
        (ahead[far],) = call(
            functools.partial(ahead_kernel, full),
            [shape((tokens, columns), F32)],
            (mine, my_weights[far]),
            cost=0.4,
        )

    blocks_out = columns // LANES
    cuts = [0, blocks_out // 4, blocks_out - blocks_out // 6, blocks_out]
    received = [[[] for _ in range(PARTS)] for _ in range(far_count)]
    reach = far_count // 2
    while reach:
        for far in range(reach, 2 * reach):
            for part, (first, end) in enumerate(zip(cuts[:-1], cuts[1:])):
                (away,) = call(
                    functools.partial(away_kernel, full, first, part == PARTS - 2),
                    [shape(((end - first) * tokens + SUBLANES * (part == PARTS - 2), LANES), BF16)],
                    (ahead[far], mine, mate, their_weights[far], *received[far][part]),
                    cost=0.2,
                )
                received[far - reach][part].append(swap(away, "head", reach << 1))
        reach //= 2
    (partial,) = call(
        functools.partial(home_kernel, full),
        [shape((tokens, columns), F32)],
        (mine, mate, my_weights[0], their_weights[0]),
        cost=0.6,
    )
    widths = [(end - first) * LANES for first, end in zip(cuts[:-1], cuts[1:])]
    scale, *done = call(
        functools.partial(middle_kernel, full, cuts[: PARTS - 1], len(received[0][0])),
        [shape((tokens, 1), F32)] + [shape((tokens, width), BF16) for width in widths[:-1]],
        (mine, mate, partial, *(other for group in received[0][:-1] for other in group)),
        cost=0.3,
    )
    (mixed,) = call(
        functools.partial(last_kernel, cuts[PARTS - 1], len(done)),
        [shape((tokens, columns), BF16)],
        (partial, scale, *done, *received[0][PARTS - 1]),
        out_places=[FAR],
        scratch=[pltpu.VMEM((tokens, widths[-1]), BF16), dma((PARTS,))],
    )
    return mixed


def solution(mesh):
    placed = (
        P("ctx", "head"),
        P("ctx", "head"),
        P("ctx", "head"),
        P("ctx", "head"),
        P("head"),
        P("head", None),
    )
    return jax.shard_map(
        local, mesh=mesh, in_specs=placed, out_specs=P("ctx", "head"), check_vma=False
    )
```

```python
import functools

import jax
import jax.numpy as jnp
from jax import lax
from jax.experimental import pallas as pl
from jax.experimental.pallas import tpu as pltpu
from jax.sharding import PartitionSpec as P

F32, BF16 = jnp.float32, jnp.bfloat16
HIGHEST = lax.Precision.HIGHEST
VMEM = pl.BlockSpec(memory_space=pltpu.VMEM)
FAR = pl.BlockSpec(memory_space=pltpu.HBM)
LANES = 128
SUBLANES = 16
PARTS = 3


def call(body, outs, operands, far=0, out_places=None, scratch=(), cost=1.0):
    held = [pltpu.with_memory_space_constraint(o, pltpu.HBM) for o in operands[:far]]
    return pl.pallas_call(
        body,
        out_shape=outs,
        in_specs=[FAR] * far + [VMEM] * (len(operands) - far),
        out_specs=out_places or [VMEM] * len(outs),
        scratch_shapes=scratch,
        cost_estimate=pl.CostEstimate(flops=int(cost * 1e9), bytes_accessed=int(cost * 1e6), transcendentals=0),
        compiler_params=pltpu.CompilerParams(vmem_limit_bytes=32 << 20),
    )(*held, *operands[far:])


def shape(dims, dtype):
    return jax.ShapeDtypeStruct(dims, dtype)


def padded(rows):
    return -(-rows // SUBLANES) * SUBLANES


def split3(value):
    high = value.astype(BF16)
    rest = value - high.astype(F32)
    mid = rest.astype(BF16)
    return high, mid, (rest - mid.astype(F32)).astype(BF16)


def stacked(value, heads):
    parts = list(split3(value))
    fill = padded(3 * heads) - 3 * heads
    if fill:
        parts.append(jnp.zeros((fill, LANES), BF16))
    return jnp.concatenate([part.astype(F32) for part in parts], axis=0).astype(BF16)


def unstacked(rows, heads):
    rows = rows.astype(F32)
    return rows[:heads] + rows[heads : 2 * heads] + rows[2 * heads : 3 * heads]


def triangle(tokens):
    row = lax.broadcasted_iota(jnp.int32, (tokens, tokens), 0)
    col = lax.broadcasted_iota(jnp.int32, (tokens, tokens), 1)
    return row, col


def column_sums(decay):
    row, col = triangle(decay.shape[1])
    lower = jnp.where(row >= col, 1.0, 0.0).astype(F32)
    return lax.dot_general(lower, decay, (((1,), (1,)), ((), ())), precision=HIGHEST)


def row_sums(decay):
    row, col = triangle(decay.shape[1])
    upper = jnp.where(row <= col, 1.0, 0.0).astype(F32)
    return jnp.dot(decay, upper, precision=HIGHEST)


def odd(axis, step=0):
    return (lax.axis_index(axis) >> step) % 2 == 1


def fetch(sources, targets, semaphores):
    copies = [
        pltpu.make_async_copy(source, target, semaphores.at[index])
        for index, (source, target) in enumerate(zip(sources, targets))
    ]
    for copy in copies:
        copy.start()
    return copies


def states_kernel(keys_far, values_far, decay_far, message, keys, values, decay, tails, semaphores):
    decay_copy, *copies = fetch((decay_far, keys_far, values_far), (decay, keys, values), semaphores)
    decay_copy.wait()
    heads, tokens = decay.shape
    width = keys.shape[1] // heads
    column = column_sums(decay[...])
    tail = jnp.exp(column[tokens - 1 : tokens, :] - column)
    for head in range(heads):
        tails[:, head * width : (head + 1) * width] = jnp.broadcast_to(tail[:, head : head + 1], (tokens, width))
    total = jnp.sum(decay[...], axis=1, keepdims=True)
    message[heads * width :, :] = stacked(jnp.broadcast_to(jnp.exp(total), (heads, LANES)), heads)
    for copy in copies:
        copy.wait()
    for head in range(heads):
        own = slice(head * width, (head + 1) * width)
        faded = (keys[:, own].astype(F32) * tails[:, own]).astype(BF16)
        state = lax.dot_general(
            faded, values[:, own], (((0,), (0,)), ((), ())), preferred_element_type=F32
        )
        message[own, :] = state.astype(BF16)


def weights_kernel(far_count, split, weight_far, _, *refs):
    *weights, token, semaphores = refs
    columns = weights[0].shape[1]
    me = lax.axis_index("head")
    copies = []

    def copy(owner, first, end, target):
        start = pl.multiple_of(owner * columns + first, LANES)
        source = weight_far.at[:, pl.ds(start, end - first)]
        copies.append(pltpu.make_async_copy(source, target.at[:, first:end], semaphores.at[len(copies)]))
        copies[-1].start()

    for index, target in enumerate(weights):
        far = far_count - 1 - index // 2
        owner = me ^ (far << 1) ^ (1 - index % 2)
        if far % 2:
            copy(owner, 0, split, target)
            copy(owner ^ 1, split, columns, target)
        else:
            copy(owner, 0, columns, target)
    token[...] = jnp.zeros_like(token)
    for one in copies:
        one.wait()


def within_kernel(step, query_far, keys_far, values_far, decay_far, before, before_decay, *refs):
    within, factor, query, keys, values, decay, semaphores = refs
    for copy in fetch((query_far, keys_far, values_far, decay_far), (query, keys, values, decay), semaphores):
        copy.wait()
    heads, tokens = decay.shape
    width = keys.shape[1] // heads
    column = column_sums(decay[...])
    line = row_sums(decay[...])
    grown = jnp.exp(column)
    scale = jnp.where(odd("ctx", step), before_decay[...], 0.0 * before_decay[...])
    row, col = triangle(tokens)
    for head in range(heads):
        own = slice(head * width, (head + 1) * width)
        scores = lax.dot_general(
            query[:, own], keys[:, own], (((1,), (1,)), ((), ())), preferred_element_type=F32
        )
        differ = jnp.where(row >= col, column[:, head : head + 1] - line[head : head + 1, :], -1e30)
        weights = (jnp.exp(differ) * scores).astype(BF16)
        carried = jnp.dot(query[:, own], before[own, :].astype(BF16), preferred_element_type=F32)
        spread = jnp.broadcast_to(grown[:, head : head + 1], (tokens, width))
        within[:, own] = jnp.dot(weights, values[:, own], preferred_element_type=F32) + spread * carried
        factor[:, own] = spread * scale[head : head + 1]


def join_kernel(step, heads, *refs):
    first = step == 0
    if first:
        mine, theirs, _, joined, entering, entering_decay = refs
    else:
        mine, theirs, before, before_decay, joined, entering, entering_decay = refs
    later = odd("ctx", step)
    rows = mine.shape[0] - padded(3 * heads)
    width = rows // heads
    my_decay = unstacked(mine[rows:, :], heads)
    their_decay = unstacked(theirs[rows:, :], heads)
    one = jnp.ones_like(my_decay)
    for_theirs = jnp.where(later, my_decay, one)
    for_mine = jnp.where(later, one, their_decay)
    if first:
        for_entering = jnp.where(later, one, 0.0 * one)
        entering_decay[...] = jnp.where(later, their_decay, one)
    else:
        for_entering = jnp.where(later, before_decay[...], 0.0 * one)
        entering_decay[...] = before_decay[...] * jnp.where(later, their_decay, one)
    for head in range(heads):
        own = slice(head * width, (head + 1) * width)
        row = slice(head, head + 1)
        received = theirs[own, :].astype(F32)
        joined[own, :] = (for_theirs[row] * received + for_mine[row] * mine[own, :].astype(F32)).astype(BF16)
        added = for_entering[row] * received
        entering[own, :] = added if first else before[own, :] + added
    if joined.shape[0] > rows:
        joined[rows:, :] = stacked(my_decay * their_decay, heads)


def attend_kernel(heads, query, within, factor, theirs, gain, message):
    tokens, full = query.shape
    width = full // heads
    squares = jnp.zeros((tokens, width), F32)
    for head in range(heads):
        own = slice(head * width, (head + 1) * width)
        carried = jnp.dot(query[:, own], theirs[own, :], preferred_element_type=F32)
        attn = within[:, own] + factor[:, own] * carried
        squares = squares + attn * attn
        message[:, own] = (attn * gain[:, own]).astype(BF16)
    squares = jnp.sum(squares, axis=1, keepdims=True)
    high, mid, low = split3(squares)
    lane = lax.broadcasted_iota(jnp.int32, (tokens, LANES), 1)
    pieces = jnp.where(lane == 0, high.astype(F32), 0.0)
    pieces = jnp.where(lane == 1, mid.astype(F32), pieces)
    message[:, full:] = jnp.where(lane == 2, low.astype(F32), pieces).astype(BF16)


def squares_row(mine, theirs, full):
    column = jnp.sum(mine[:, full:].astype(F32) + theirs[:, full:].astype(F32), axis=1, keepdims=True)
    row, col = triangle(mine.shape[0])
    return jnp.sum(jnp.where(row == col, column, 0.0), axis=0, keepdims=True)


def ahead_kernel(full, mine, weight, result):
    result[...] = jnp.dot(mine[:, :full], weight[...], preferred_element_type=F32)


def away_kernel(full, first_block, leading, partial, mine, theirs, their_weight, *refs):
    *received, message = refs
    tokens = mine.shape[0]
    blocks = message.shape[0] // tokens
    columns = slice(first_block * LANES, (first_block + blocks) * LANES)
    result = partial[:, columns] + jnp.dot(theirs[:, :full], their_weight[:, columns], preferred_element_type=F32)
    for block in range(blocks):
        there = slice(block * tokens, (block + 1) * tokens)
        part = result[:, block * LANES : (block + 1) * LANES]
        for other in received:
            part = part + other[there, :].astype(F32)
        message[there, :] = part.astype(BF16)
    if leading:
        total = squares_row(mine, theirs, full)
        for other in received:
            total = total + unstacked(other[blocks * tokens :, :], 1)
        message[blocks * tokens :, :] = stacked(total, 1)


def home_kernel(full, mine, theirs, my_weight, their_weight, result):
    result[...] = jnp.dot(mine[:, :full], my_weight[...], preferred_element_type=F32) + jnp.dot(
        theirs[:, :full], their_weight[...], preferred_element_type=F32
    )


def scaled(partial, first_block, received, scale, out):
    tokens, columns = out.shape
    for block in range(columns // LANES):
        summed = partial[:, (first_block + block) * LANES : (first_block + block + 1) * LANES]
        for other in received:
            summed = summed + other[block * tokens : (block + 1) * tokens, :].astype(F32)
        out[:, block * LANES : (block + 1) * LANES] = (summed * scale).astype(BF16)


def middle_kernel(full, cuts, count, mine, theirs, partial, *refs):
    received, (scale, *outs) = refs[: len(cuts) * count], refs[len(cuts) * count :]
    groups = [received[part * count : (part + 1) * count] for part in range(len(cuts))]
    total = squares_row(mine, theirs, full)
    for other in groups[-1]:
        total = total + unstacked(other[other.shape[0] - SUBLANES :, :], 1)
    row, col = triangle(mine.shape[0])
    total = jnp.sum(jnp.where(row == col, total, 0.0), axis=1, keepdims=True)
    factor = lax.rsqrt(total / (full * lax.axis_size("head")) + 1e-05)
    scale[...] = factor
    for first_block, group, out in zip(cuts, groups, outs):
        scaled(partial, first_block, group, factor, out)


def last_kernel(first_block, done_count, partial, scale, *refs):
    done, received = refs[:done_count], refs[done_count:-3]
    out, staged, semaphores = refs[-3:]
    copies = []

    def write(source, column):
        there = out.at[:, column : column + source.shape[1]]
        copies.append(pltpu.make_async_copy(source, there, semaphores.at[len(copies)]))
        copies[-1].start()

    column = 0
    for part in done:
        write(part, column)
        column += part.shape[1]
    scaled(partial, first_block, received, scale[...], staged)
    write(staged, column)
    for copy in copies:
        copy.wait()


def local(query, keys, values, log_decay, norm_gain, out_weight):
    tokens, full = query.shape
    heads = log_decay.shape[1]
    steps = lax.axis_size("ctx").bit_length() - 1
    groups = lax.axis_size("head")
    columns = out_weight.shape[1] // groups
    decay = log_decay.T
    message_shape = shape((full + padded(3 * heads), LANES), BF16)
    dma = pltpu.SemaphoreType.DMA

    def swap(value, axis, bit):
        count = lax.axis_size(axis)
        return lax.ppermute(value, axis, [(i, i ^ bit) for i in range(count)])

    blocks = [pltpu.VMEM(array.shape, array.dtype) for array in (query, keys, values, decay)]
    (message,) = call(
        states_kernel,
        [message_shape],
        (keys, values, decay),
        far=3,
        scratch=[*blocks[1:], pltpu.VMEM((tokens, full), F32), dma((3,))],
    )
    theirs = swap(message, "ctx", 1)

    far_count = groups // 2
    blocks_out = columns // LANES
    cuts = [0, blocks_out // 4, blocks_out - blocks_out // 4, blocks_out]
    *weights, token = call(
        functools.partial(weights_kernel, far_count, cuts[-2] * LANES),
        [shape((full, columns), BF16)] * (2 * far_count) + [shape((8, LANES), F32)],
        (out_weight, message),
        far=1,
        scratch=[dma((3 * far_count,))],
        cost=2.0,
    )
    my_weights, their_weights = {}, {}
    for index in range(0, 2 * far_count, 2):
        far = far_count - 1 - index // 2
        their_weights[far] = swap(weights[index], "head", 1)
        my_weights[far] = weights[index + 1]

    entering = (token,)
    for step in range(steps - 1):
        message, *entering = call(
            functools.partial(join_kernel, step, heads),
            [
                message_shape if step < steps - 2 else shape((full, LANES), BF16),
                shape((full, LANES), F32),
                shape((heads, LANES), F32),
            ],
            (message, theirs, *entering),
            cost=30.0 if step == steps - 2 else 0.1,
        )
        theirs = swap(message, "ctx", 2 << step)
    within, factor = call(
        functools.partial(within_kernel, steps - 1),
        [shape((tokens, full), F32)] * 2,
        (query, keys, values, decay, *entering),
        far=4,
        scratch=[*blocks, dma((4,))],
        cost=1.0,
    )
    (mine,) = call(
        functools.partial(attend_kernel, heads),
        [shape((tokens, full + LANES), BF16)],
        (query, within, factor, theirs, norm_gain[None, :]),
    )
    mate = swap(mine, "head", 1)
    ahead = {}
    for far in range(1, far_count):
        (ahead[far],) = call(
            functools.partial(ahead_kernel, full),
            [shape((tokens, columns), F32)],
            (mine, my_weights[far]),
            cost=0.4,
        )

    received = [[[] for _ in range(PARTS)] for _ in range(far_count)]
    reach = far_count // 2
    while reach:
        for far in range(reach, 2 * reach):
            for part, (first, end) in enumerate(zip(cuts[:-1], cuts[1:])):
                (away,) = call(
                    functools.partial(away_kernel, full, first, part == PARTS - 2),
                    [shape(((end - first) * tokens + SUBLANES * (part == PARTS - 2), LANES), BF16)],
                    (ahead[far], mine, mate, their_weights[far], *received[far][part]),
                    cost=0.2,
                )
                hop = 3 if reach == 1 and part == PARTS - 1 else reach << 1
                received[far - reach][part].append(swap(away, "head", hop))
        reach //= 2
    (partial,) = call(
        functools.partial(home_kernel, full),
        [shape((tokens, columns), F32)],
        (mine, mate, my_weights[0], their_weights[0]),
        cost=0.6,
    )
    widths = [(end - first) * LANES for first, end in zip(cuts[:-1], cuts[1:])]
    scale, *done = call(
        functools.partial(middle_kernel, full, cuts[: PARTS - 1], len(received[0][0])),
        [shape((tokens, 1), F32)] + [shape((tokens, width), BF16) for width in widths[:-1]],
        (mine, mate, partial, *(other for group in received[0][:-1] for other in group)),
        cost=0.3,
    )
    (mixed,) = call(
        functools.partial(last_kernel, cuts[PARTS - 1], len(done)),
        [shape((tokens, columns), BF16)],
        (partial, scale, *done, *received[0][PARTS - 1]),
        out_places=[FAR],
        scratch=[pltpu.VMEM((tokens, widths[-1]), BF16), dma((PARTS,))],
    )
    return mixed


def solution(mesh):
    placed = (
        P("ctx", "head"),
        P("ctx", "head"),
        P("ctx", "head"),
        P("ctx", "head"),
        P("head"),
        P("head", None),
    )
    return jax.shard_map(
        local, mesh=mesh, in_specs=placed, out_specs=P("ctx", "head"), check_vma=False
    )
```

```python
import functools

import jax
import jax.numpy as jnp
from jax import lax
from jax.experimental import pallas as pl
from jax.experimental.pallas import tpu as pltpu
from jax.sharding import PartitionSpec as P

F32, BF16 = jnp.float32, jnp.bfloat16
HIGHEST = lax.Precision.HIGHEST
VMEM = pl.BlockSpec(memory_space=pltpu.VMEM)
FAR = pl.BlockSpec(memory_space=pltpu.HBM)
LANES = 128
SUBLANES = 16
PARTS = 3


def call(body, outs, operands, far=0, out_places=None, scratch=(), cost=1.0):
    held = [pltpu.with_memory_space_constraint(o, pltpu.HBM) for o in operands[:far]]
    return pl.pallas_call(
        body,
        out_shape=outs,
        in_specs=[FAR] * far + [VMEM] * (len(operands) - far),
        out_specs=out_places or [VMEM] * len(outs),
        scratch_shapes=scratch,
        cost_estimate=pl.CostEstimate(flops=int(cost * 1e9), bytes_accessed=int(cost * 1e6), transcendentals=0),
        compiler_params=pltpu.CompilerParams(vmem_limit_bytes=32 << 20),
    )(*held, *operands[far:])


def shape(dims, dtype):
    return jax.ShapeDtypeStruct(dims, dtype)


def padded(rows):
    return -(-rows // SUBLANES) * SUBLANES


def split3(value):
    high = value.astype(BF16)
    rest = value - high.astype(F32)
    mid = rest.astype(BF16)
    return high, mid, (rest - mid.astype(F32)).astype(BF16)


def stacked(value, heads):
    parts = list(split3(value))
    fill = padded(3 * heads) - 3 * heads
    if fill:
        parts.append(jnp.zeros((fill, LANES), BF16))
    return jnp.concatenate([part.astype(F32) for part in parts], axis=0).astype(BF16)


def unstacked(rows, heads):
    rows = rows.astype(F32)
    return rows[:heads] + rows[heads : 2 * heads] + rows[2 * heads : 3 * heads]


def triangle(tokens):
    row = lax.broadcasted_iota(jnp.int32, (tokens, tokens), 0)
    col = lax.broadcasted_iota(jnp.int32, (tokens, tokens), 1)
    return row, col


def column_sums(decay):
    heads, tokens = decay.shape
    row, col = triangle(tokens)
    lower = jnp.where(row >= col, 1.0, 0.0).astype(BF16)
    sums = [
        lax.dot_general(lower, part, (((1,), (1,)), ((), ())), preferred_element_type=F32) for part in split3(decay)
    ]
    return sums[0] + (sums[1] + sums[2])


def row_sums(decay):
    row, col = triangle(decay.shape[1])
    upper = jnp.where(row <= col, 1.0, 0.0).astype(F32)
    return jnp.dot(decay, upper, precision=HIGHEST)


def odd(axis, step=0):
    return (lax.axis_index(axis) >> step) % 2 == 1


def fetch(sources, targets, semaphores):
    copies = [
        pltpu.make_async_copy(source, target, semaphores.at[index])
        for index, (source, target) in enumerate(zip(sources, targets))
    ]
    for copy in copies:
        copy.start()
    return copies


def states_kernel(keys_far, values_far, decay_far, message, keys, values, decay, tails, semaphores):
    decay_copy, *copies = fetch((decay_far, keys_far, values_far), (decay, keys, values), semaphores)
    decay_copy.wait()
    heads, tokens = decay.shape
    width = keys.shape[1] // heads
    column = column_sums(decay[...])
    tail = jnp.exp(column[tokens - 1 : tokens, :] - column)
    for head in range(heads):
        tails[:, head * width : (head + 1) * width] = jnp.broadcast_to(tail[:, head : head + 1], (tokens, width))
    total = jnp.sum(decay[...], axis=1, keepdims=True)
    message[heads * width :, :] = stacked(jnp.broadcast_to(jnp.exp(total), (heads, LANES)), heads)
    for copy in copies:
        copy.wait()
    for head in range(heads):
        own = slice(head * width, (head + 1) * width)
        faded = (values[:, own].astype(F32) * tails[:, own]).astype(BF16)
        state = lax.dot_general(
            keys[:, own], faded, (((0,), (0,)), ((), ())), preferred_element_type=F32
        )
        message[own, :] = state.astype(BF16)


def weights_kernel(far_count, split, weight_far, _, *refs):
    *weights, token, semaphores = refs
    columns = weights[0].shape[1]
    me = lax.axis_index("head")
    copies = []

    def copy(owner, first, end, target):
        start = pl.multiple_of(owner * columns + first, LANES)
        source = weight_far.at[:, pl.ds(start, end - first)]
        copies.append(pltpu.make_async_copy(source, target.at[:, first:end], semaphores.at[len(copies)]))
        copies[-1].start()

    for index, target in enumerate(weights):
        far = far_count - 1 - index // 2
        owner = me ^ (far << 1) ^ (1 - index % 2)
        if far % 2:
            copy(owner, 0, split, target)
            copy(owner ^ 1, split, columns, target)
        else:
            copy(owner, 0, columns, target)
    token[...] = jnp.zeros_like(token)
    for one in copies:
        one.wait()


def within_kernel(step, query_far, keys_far, values_far, decay_far, before, before_decay, *refs):
    within, factor, query, keys, values, decay, semaphores = refs
    for copy in fetch((query_far, keys_far, values_far, decay_far), (query, keys, values, decay), semaphores):
        copy.wait()
    heads, tokens = decay.shape
    width = keys.shape[1] // heads
    column = column_sums(decay[...])
    line = row_sums(decay[...])
    grown = jnp.exp(column)
    scale = jnp.where(odd("ctx", step), before_decay[...], 0.0 * before_decay[...])
    row, col = triangle(tokens)
    for head in range(heads):
        own = slice(head * width, (head + 1) * width)
        scores = lax.dot_general(
            query[:, own], keys[:, own], (((1,), (1,)), ((), ())), preferred_element_type=F32
        )
        differ = jnp.where(row >= col, column[:, head : head + 1] - line[head : head + 1, :], -1e30)
        weights = (jnp.exp(differ) * scores).astype(BF16)
        carried = jnp.dot(query[:, own], before[own, :].astype(BF16), preferred_element_type=F32)
        spread = jnp.broadcast_to(grown[:, head : head + 1], (tokens, width))
        within[:, own] = jnp.dot(weights, values[:, own], preferred_element_type=F32) + spread * carried
        factor[:, own] = spread * scale[head : head + 1]


def join_kernel(step, heads, *refs):
    first = step == 0
    if first:
        mine, theirs, _, joined, entering, entering_decay = refs
    else:
        mine, theirs, before, before_decay, joined, entering, entering_decay = refs
    later = odd("ctx", step)
    rows = mine.shape[0] - padded(3 * heads)
    width = rows // heads
    my_decay = unstacked(mine[rows:, :], heads)
    their_decay = unstacked(theirs[rows:, :], heads)
    one = jnp.ones_like(my_decay)
    for_theirs = jnp.where(later, my_decay, one)
    for_mine = jnp.where(later, one, their_decay)
    if first:
        for_entering = jnp.where(later, one, 0.0 * one)
        entering_decay[...] = jnp.where(later, their_decay, one)
    else:
        for_entering = jnp.where(later, before_decay[...], 0.0 * one)
        entering_decay[...] = before_decay[...] * jnp.where(later, their_decay, one)
    for head in range(heads):
        own = slice(head * width, (head + 1) * width)
        row = slice(head, head + 1)
        received = theirs[own, :].astype(F32)
        joined[own, :] = (for_theirs[row] * received + for_mine[row] * mine[own, :].astype(F32)).astype(BF16)
        added = for_entering[row] * received
        entering[own, :] = added if first else before[own, :] + added
    if joined.shape[0] > rows:
        joined[rows:, :] = stacked(my_decay * their_decay, heads)


def attend_kernel(heads, query, within, factor, theirs, gain, message):
    tokens, full = query.shape
    width = full // heads
    squares = jnp.zeros((tokens, width), F32)
    for head in range(heads):
        own = slice(head * width, (head + 1) * width)
        carried = jnp.dot(query[:, own], theirs[own, :], preferred_element_type=F32)
        attn = within[:, own] + factor[:, own] * carried
        squares = squares + attn * attn
        message[:, own] = (attn * gain[:, own]).astype(BF16)
    squares = jnp.sum(squares, axis=1, keepdims=True)
    high, mid, low = split3(squares)
    lane = lax.broadcasted_iota(jnp.int32, (tokens, LANES), 1)
    pieces = jnp.where(lane == 0, high.astype(F32), 0.0)
    pieces = jnp.where(lane == 1, mid.astype(F32), pieces)
    message[:, full:] = jnp.where(lane == 2, low.astype(F32), pieces).astype(BF16)


def squares_row(mine, theirs, full):
    column = jnp.sum(mine[:, full:].astype(F32) + theirs[:, full:].astype(F32), axis=1, keepdims=True)
    row, col = triangle(mine.shape[0])
    return jnp.sum(jnp.where(row == col, column, 0.0), axis=0, keepdims=True)


def ahead_kernel(full, mine, weight, result):
    result[...] = jnp.dot(mine[:, :full], weight[...], preferred_element_type=F32)


def away_kernel(full, first_block, leading, partial, mine, theirs, their_weight, *refs):
    *received, message = refs
    tokens = mine.shape[0]
    blocks = message.shape[0] // tokens
    columns = slice(first_block * LANES, (first_block + blocks) * LANES)
    result = partial[:, columns] + jnp.dot(theirs[:, :full], their_weight[:, columns], preferred_element_type=F32)
    for block in range(blocks):
        there = slice(block * tokens, (block + 1) * tokens)
        part = result[:, block * LANES : (block + 1) * LANES]
        for other in received:
            part = part + other[there, :].astype(F32)
        message[there, :] = part.astype(BF16)
    if leading:
        total = squares_row(mine, theirs, full)
        for other in received:
            total = total + unstacked(other[blocks * tokens :, :], 1)
        message[blocks * tokens :, :] = stacked(total, 1)


def home_kernel(full, mine, theirs, my_weight, their_weight, result):
    result[...] = jnp.dot(mine[:, :full], my_weight[...], preferred_element_type=F32) + jnp.dot(
        theirs[:, :full], their_weight[...], preferred_element_type=F32
    )


def scaled(partial, first_block, received, scale, out):
    tokens, columns = out.shape
    for block in range(columns // LANES):
        summed = partial[:, (first_block + block) * LANES : (first_block + block + 1) * LANES]
        for other in received:
            summed = summed + other[block * tokens : (block + 1) * tokens, :].astype(F32)
        out[:, block * LANES : (block + 1) * LANES] = (summed * scale).astype(BF16)


def middle_kernel(full, cuts, count, mine, theirs, partial, *refs):
    received, (scale, *outs) = refs[: len(cuts) * count], refs[len(cuts) * count :]
    groups = [received[part * count : (part + 1) * count] for part in range(len(cuts))]
    total = squares_row(mine, theirs, full)
    for other in groups[-1]:
        total = total + unstacked(other[other.shape[0] - SUBLANES :, :], 1)
    row, col = triangle(mine.shape[0])
    total = jnp.sum(jnp.where(row == col, total, 0.0), axis=1, keepdims=True)
    factor = lax.rsqrt(total / (full * lax.axis_size("head")) + 1e-05)
    scale[...] = factor
    for first_block, group, out in zip(cuts, groups, outs):
        scaled(partial, first_block, group, factor, out)


def last_kernel(first_block, done_count, partial, scale, *refs):
    done, received = refs[:done_count], refs[done_count:-3]
    out, staged, semaphores = refs[-3:]
    copies = []

    def write(source, column):
        there = out.at[:, column : column + source.shape[1]]
        copies.append(pltpu.make_async_copy(source, there, semaphores.at[len(copies)]))
        copies[-1].start()

    column = 0
    for part in done:
        write(part, column)
        column += part.shape[1]
    scaled(partial, first_block, received, scale[...], staged)
    write(staged, column)
    for copy in copies:
        copy.wait()


def local(query, keys, values, log_decay, norm_gain, out_weight):
    tokens, full = query.shape
    heads = log_decay.shape[1]
    steps = lax.axis_size("ctx").bit_length() - 1
    groups = lax.axis_size("head")
    columns = out_weight.shape[1] // groups
    decay = log_decay.T
    message_shape = shape((full + padded(3 * heads), LANES), BF16)
    dma = pltpu.SemaphoreType.DMA

    def swap(value, axis, bit):
        count = lax.axis_size(axis)
        return lax.ppermute(value, axis, [(i, i ^ bit) for i in range(count)])

    blocks = [pltpu.VMEM(array.shape, array.dtype) for array in (query, keys, values, decay)]
    (message,) = call(
        states_kernel,
        [message_shape],
        (keys, values, decay),
        far=3,
        scratch=[*blocks[1:], pltpu.VMEM((tokens, full), F32), dma((3,))],
    )
    theirs = swap(message, "ctx", 1)

    far_count = groups // 2
    blocks_out = columns // LANES
    cuts = [0, blocks_out // 3, blocks_out - blocks_out // 4, blocks_out]
    *weights, token = call(
        functools.partial(weights_kernel, far_count, cuts[-2] * LANES),
        [shape((full, columns), BF16)] * (2 * far_count) + [shape((8, LANES), F32)],
        (out_weight, message),
        far=1,
        scratch=[dma((3 * far_count,))],
        cost=2.0,
    )
    my_weights, their_weights = {}, {}
    for index in range(0, 2 * far_count, 2):
        far = far_count - 1 - index // 2
        their_weights[far] = swap(weights[index], "head", 1)
        my_weights[far] = weights[index + 1]

    entering = (token,)
    for step in range(steps - 1):
        message, *entering = call(
            functools.partial(join_kernel, step, heads),
            [
                message_shape if step < steps - 2 else shape((full, LANES), BF16),
                shape((full, LANES), F32),
                shape((heads, LANES), F32),
            ],
            (message, theirs, *entering),
            cost=30.0 if step == steps - 2 else 0.1,
        )
        theirs = swap(message, "ctx", 2 << step)
    within, factor = call(
        functools.partial(within_kernel, steps - 1),
        [shape((tokens, full), F32)] * 2,
        (query, keys, values, decay, *entering),
        far=4,
        scratch=[*blocks, dma((4,))],
        cost=1.0,
    )
    (mine,) = call(
        functools.partial(attend_kernel, heads),
        [shape((tokens, full + LANES), BF16)],
        (query, within, factor, theirs, norm_gain[None, :]),
    )
    mate = swap(mine, "head", 1)
    ahead = {}
    for far in range(1, far_count):
        (ahead[far],) = call(
            functools.partial(ahead_kernel, full),
            [shape((tokens, columns), F32)],
            (mine, my_weights[far]),
            cost=0.4,
        )

    received = [[[] for _ in range(PARTS)] for _ in range(far_count)]
    reach = far_count // 2
    while reach:
        for far in range(reach, 2 * reach):
            for part, (first, end) in enumerate(zip(cuts[:-1], cuts[1:])):
                (away,) = call(
                    functools.partial(away_kernel, full, first, part == PARTS - 2),
                    [shape(((end - first) * tokens + SUBLANES * (part == PARTS - 2), LANES), BF16)],
                    (ahead[far], mine, mate, their_weights[far], *received[far][part]),
                    cost=0.2,
                )
                hop = 3 if reach == 1 and part == PARTS - 1 else reach << 1
                received[far - reach][part].append(swap(away, "head", hop))
        reach //= 2
    (partial,) = call(
        functools.partial(home_kernel, full),
        [shape((tokens, columns), F32)],
        (mine, mate, my_weights[0], their_weights[0]),
        cost=0.6,
    )
    widths = [(end - first) * LANES for first, end in zip(cuts[:-1], cuts[1:])]
    scale, *done = call(
        functools.partial(middle_kernel, full, cuts[: PARTS - 1], len(received[0][0])),
        [shape((tokens, 1), F32)] + [shape((tokens, width), BF16) for width in widths[:-1]],
        (mine, mate, partial, *(other for group in received[0][:-1] for other in group)),
        cost=0.3,
    )
    (mixed,) = call(
        functools.partial(last_kernel, cuts[PARTS - 1], len(done)),
        [shape((tokens, columns), BF16)],
        (partial, scale, *done, *received[0][PARTS - 1]),
        out_places=[FAR],
        scratch=[pltpu.VMEM((tokens, widths[-1]), BF16), dma((PARTS,))],
    )
    return mixed


def solution(mesh):
    placed = (
        P("ctx", "head"),
        P("ctx", "head"),
        P("ctx", "head"),
        P("ctx", "head"),
        P("head"),
        P("head", None),
    )
    return jax.shard_map(
        local, mesh=mesh, in_specs=placed, out_specs=P("ctx", "head"), check_vma=False
    )
```

```python
import functools

import jax
import jax.numpy as jnp
from jax import lax
from jax.experimental import pallas as pl
from jax.experimental.pallas import tpu as pltpu
from jax.sharding import PartitionSpec as P

F32, BF16 = jnp.float32, jnp.bfloat16
HIGHEST = lax.Precision.HIGHEST
VMEM = pl.BlockSpec(memory_space=pltpu.VMEM)
FAR = pl.BlockSpec(memory_space=pltpu.HBM)
LANES = 128
SUBLANES = 16
PARTS = 3


def call(body, outs, operands, far=0, out_places=None, scratch=(), cost=1.0):
    held = [pltpu.with_memory_space_constraint(o, pltpu.HBM) for o in operands[:far]]
    return pl.pallas_call(
        body,
        out_shape=outs,
        in_specs=[FAR] * far + [VMEM] * (len(operands) - far),
        out_specs=out_places or [VMEM] * len(outs),
        scratch_shapes=scratch,
        cost_estimate=pl.CostEstimate(flops=int(cost * 1e9), bytes_accessed=int(cost * 1e6), transcendentals=0),
        compiler_params=pltpu.CompilerParams(vmem_limit_bytes=32 << 20),
    )(*held, *operands[far:])


def shape(dims, dtype):
    return jax.ShapeDtypeStruct(dims, dtype)


def padded(rows):
    return -(-rows // SUBLANES) * SUBLANES


def split3(value):
    high = value.astype(BF16)
    rest = value - high.astype(F32)
    mid = rest.astype(BF16)
    return high, mid, (rest - mid.astype(F32)).astype(BF16)


def stacked(value, heads):
    parts = list(split3(value))
    fill = padded(3 * heads) - 3 * heads
    if fill:
        parts.append(jnp.zeros((fill, LANES), BF16))
    return jnp.concatenate([part.astype(F32) for part in parts], axis=0).astype(BF16)


def unstacked(rows, heads):
    rows = rows.astype(F32)
    return rows[:heads] + rows[heads : 2 * heads] + rows[2 * heads : 3 * heads]


def triangle(tokens):
    row = lax.broadcasted_iota(jnp.int32, (tokens, tokens), 0)
    col = lax.broadcasted_iota(jnp.int32, (tokens, tokens), 1)
    return row, col


def column_sums(decay):
    heads, tokens = decay.shape
    row, col = triangle(tokens)
    lower = jnp.where(row >= col, 1.0, 0.0).astype(BF16)
    sums = [
        lax.dot_general(lower, part, (((1,), (1,)), ((), ())), preferred_element_type=F32) for part in split3(decay)
    ]
    return sums[0] + (sums[1] + sums[2])


def row_sums(decay):
    row, col = triangle(decay.shape[1])
    upper = jnp.where(row <= col, 1.0, 0.0).astype(F32)
    return jnp.dot(decay, upper, precision=HIGHEST)


def odd(axis, step=0):
    return (lax.axis_index(axis) >> step) % 2 == 1


def fetch(sources, targets, semaphores):
    copies = [
        pltpu.make_async_copy(source, target, semaphores.at[index])
        for index, (source, target) in enumerate(zip(sources, targets))
    ]
    for copy in copies:
        copy.start()
    return copies


def states_kernel(keys_far, values_far, decay_far, message, keys, values, decay, tails, semaphores):
    decay_copy, *copies = fetch((decay_far, keys_far, values_far), (decay, keys, values), semaphores)
    decay_copy.wait()
    heads, tokens = decay.shape
    width = keys.shape[1] // heads
    column = column_sums(decay[...])
    tail = jnp.exp(column[tokens - 1 : tokens, :] - column)
    for head in range(heads):
        tails[:, head * width : (head + 1) * width] = jnp.broadcast_to(tail[:, head : head + 1], (tokens, width))
    total = jnp.sum(decay[...], axis=1, keepdims=True)
    message[heads * width :, :] = stacked(jnp.broadcast_to(jnp.exp(total), (heads, LANES)), heads)
    for copy in copies:
        copy.wait()
    for head in range(heads):
        own = slice(head * width, (head + 1) * width)
        faded = (values[:, own].astype(F32) * tails[:, own]).astype(BF16)
        state = lax.dot_general(
            keys[:, own], faded, (((0,), (0,)), ((), ())), preferred_element_type=F32
        )
        message[own, :] = state.astype(BF16)


def weights_kernel(far_count, split, weight_far, _, *refs):
    *weights, token, semaphores = refs
    columns = weights[0].shape[1]
    me = lax.axis_index("head")
    copies = []

    def copy(owner, first, end, target):
        start = pl.multiple_of(owner * columns + first, LANES)
        source = weight_far.at[:, pl.ds(start, end - first)]
        copies.append(pltpu.make_async_copy(source, target.at[:, first:end], semaphores.at[len(copies)]))
        copies[-1].start()

    for index, target in enumerate(weights):
        far = far_count - 1 - index // 2
        owner = me ^ (far << 1) ^ (1 - index % 2)
        if far % 2:
            copy(owner, 0, split, target)
            copy(owner ^ 1, split, columns, target)
        else:
            copy(owner, 0, columns, target)
    token[...] = jnp.zeros_like(token)
    for one in copies:
        one.wait()


def within_kernel(step, query_far, keys_far, values_far, decay_far, before, before_decay, *refs):
    within, factor, query, keys, values, decay, semaphores = refs
    for copy in fetch((query_far, keys_far, values_far, decay_far), (query, keys, values, decay), semaphores):
        copy.wait()
    heads, tokens = decay.shape
    width = keys.shape[1] // heads
    column = column_sums(decay[...])
    line = row_sums(decay[...])
    grown = jnp.exp(column)
    scale = jnp.where(odd("ctx", step), before_decay[...], 0.0 * before_decay[...])
    row, col = triangle(tokens)
    for head in range(heads):
        own = slice(head * width, (head + 1) * width)
        scores = lax.dot_general(
            query[:, own], keys[:, own], (((1,), (1,)), ((), ())), preferred_element_type=F32
        )
        differ = jnp.where(row >= col, column[:, head : head + 1] - line[head : head + 1, :], -1e30)
        weights = (jnp.exp(differ) * scores).astype(BF16)
        carried = jnp.dot(query[:, own], before[own, :].astype(BF16), preferred_element_type=F32)
        spread = jnp.broadcast_to(grown[:, head : head + 1], (tokens, width))
        within[:, own] = jnp.dot(weights, values[:, own], preferred_element_type=F32) + spread * carried
        factor[:, own] = spread * scale[head : head + 1]


def join_kernel(step, heads, *refs):
    first = step == 0
    if first:
        mine, theirs, _, joined, entering, entering_decay = refs
    else:
        mine, theirs, before, before_decay, joined, entering, entering_decay = refs
    later = odd("ctx", step)
    rows = mine.shape[0] - padded(3 * heads)
    width = rows // heads
    my_decay = unstacked(mine[rows:, :], heads)
    their_decay = unstacked(theirs[rows:, :], heads)
    one = jnp.ones_like(my_decay)
    for_theirs = jnp.where(later, my_decay, one)
    for_mine = jnp.where(later, one, their_decay)
    if first:
        for_entering = jnp.where(later, one, 0.0 * one)
        entering_decay[...] = jnp.where(later, their_decay, one)
    else:
        for_entering = jnp.where(later, before_decay[...], 0.0 * one)
        entering_decay[...] = before_decay[...] * jnp.where(later, their_decay, one)
    for head in range(heads):
        own = slice(head * width, (head + 1) * width)
        row = slice(head, head + 1)
        received = theirs[own, :].astype(F32)
        joined[own, :] = (for_theirs[row] * received + for_mine[row] * mine[own, :].astype(F32)).astype(BF16)
        added = for_entering[row] * received
        entering[own, :] = added if first else before[own, :] + added
    if joined.shape[0] > rows:
        joined[rows:, :] = stacked(my_decay * their_decay, heads)


def attend_kernel(heads, query, within, factor, theirs, gain, message):
    tokens, full = query.shape
    width = full // heads
    squares = jnp.zeros((tokens, width), F32)
    for head in range(heads):
        own = slice(head * width, (head + 1) * width)
        carried = jnp.dot(query[:, own], theirs[own, :], preferred_element_type=F32)
        attn = within[:, own] + factor[:, own] * carried
        squares = squares + attn * attn
        message[:, own] = (attn * gain[:, own]).astype(BF16)
    message[:, full:] = squares.astype(BF16)


def squares_row(mine, theirs, full):
    column = jnp.sum(mine[:, full:].astype(F32) + theirs[:, full:].astype(F32), axis=1, keepdims=True)
    row, col = triangle(mine.shape[0])
    return jnp.sum(jnp.where(row == col, column, 0.0), axis=0, keepdims=True)


def ahead_kernel(full, mine, weight, result):
    result[...] = jnp.dot(mine[:, :full], weight[...], preferred_element_type=F32)


def away_kernel(full, first_block, leading, partial, mine, theirs, their_weight, *refs):
    *received, message = refs
    tokens = mine.shape[0]
    blocks = message.shape[0] // tokens
    columns = slice(first_block * LANES, (first_block + blocks) * LANES)
    result = partial[:, columns] + jnp.dot(theirs[:, :full], their_weight[:, columns], preferred_element_type=F32)
    for block in range(blocks):
        there = slice(block * tokens, (block + 1) * tokens)
        part = result[:, block * LANES : (block + 1) * LANES]
        for other in received:
            part = part + other[there, :].astype(F32)
        message[there, :] = part.astype(BF16)
    if leading:
        total = squares_row(mine, theirs, full)
        for other in received:
            total = total + unstacked(other[blocks * tokens :, :], 1)
        message[blocks * tokens :, :] = stacked(total, 1)


def home_kernel(full, mine, theirs, my_weight, their_weight, result):
    result[...] = jnp.dot(mine[:, :full], my_weight[...], preferred_element_type=F32) + jnp.dot(
        theirs[:, :full], their_weight[...], preferred_element_type=F32
    )


def scaled(partial, first_block, received, scale, out):
    tokens, columns = out.shape
    for block in range(columns // LANES):
        summed = partial[:, (first_block + block) * LANES : (first_block + block + 1) * LANES]
        for other in received:
            summed = summed + other[block * tokens : (block + 1) * tokens, :].astype(F32)
        out[:, block * LANES : (block + 1) * LANES] = (summed * scale).astype(BF16)


def middle_kernel(full, cuts, count, mine, theirs, partial, *refs):
    received, (scale, *outs) = refs[: len(cuts) * count], refs[len(cuts) * count :]
    groups = [received[part * count : (part + 1) * count] for part in range(len(cuts))]
    total = squares_row(mine, theirs, full)
    for other in groups[-1]:
        total = total + unstacked(other[other.shape[0] - SUBLANES :, :], 1)
    row, col = triangle(mine.shape[0])
    total = jnp.sum(jnp.where(row == col, total, 0.0), axis=1, keepdims=True)
    factor = lax.rsqrt(total / (full * lax.axis_size("head")) + 1e-05)
    scale[...] = factor
    for first_block, group, out in zip(cuts, groups, outs):
        scaled(partial, first_block, group, factor, out)


def last_kernel(first_block, done_count, partial, scale, *refs):
    done, received = refs[:done_count], refs[done_count:-3]
    out, staged, semaphores = refs[-3:]
    copies = []

    def write(source, column):
        there = out.at[:, column : column + source.shape[1]]
        copies.append(pltpu.make_async_copy(source, there, semaphores.at[len(copies)]))
        copies[-1].start()

    column = 0
    for part in done:
        write(part, column)
        column += part.shape[1]
    scaled(partial, first_block, received, scale[...], staged)
    write(staged, column)
    for copy in copies:
        copy.wait()


def local(query, keys, values, log_decay, norm_gain, out_weight):
    tokens, full = query.shape
    heads = log_decay.shape[1]
    steps = lax.axis_size("ctx").bit_length() - 1
    groups = lax.axis_size("head")
    columns = out_weight.shape[1] // groups
    decay = log_decay.T
    message_shape = shape((full + padded(3 * heads), LANES), BF16)
    dma = pltpu.SemaphoreType.DMA

    def swap(value, axis, bit):
        count = lax.axis_size(axis)
        return lax.ppermute(value, axis, [(i, i ^ bit) for i in range(count)])

    blocks = [pltpu.VMEM(array.shape, array.dtype) for array in (query, keys, values, decay)]
    (message,) = call(
        states_kernel,
        [message_shape],
        (keys, values, decay),
        far=3,
        scratch=[*blocks[1:], pltpu.VMEM((tokens, full), F32), dma((3,))],
    )
    theirs = swap(message, "ctx", 1)

    far_count = groups // 2
    blocks_out = columns // LANES
    cuts = [0, blocks_out // 3, blocks_out - blocks_out // 4, blocks_out]
    *weights, token = call(
        functools.partial(weights_kernel, far_count, cuts[-2] * LANES),
        [shape((full, columns), BF16)] * (2 * far_count) + [shape((8, LANES), F32)],
        (out_weight, message),
        far=1,
        scratch=[dma((3 * far_count,))],
        cost=2.0,
    )
    my_weights, their_weights = {}, {}
    for index in range(0, 2 * far_count, 2):
        far = far_count - 1 - index // 2
        their_weights[far] = swap(weights[index], "head", 1)
        my_weights[far] = weights[index + 1]

    entering = (token,)
    for step in range(steps - 1):
        message, *entering = call(
            functools.partial(join_kernel, step, heads),
            [
                message_shape if step < steps - 2 else shape((full, LANES), BF16),
                shape((full, LANES), F32),
                shape((heads, LANES), F32),
            ],
            (message, theirs, *entering),
            cost=30.0 if step == steps - 2 else 0.1,
        )
        theirs = swap(message, "ctx", 2 << step)
    within, factor = call(
        functools.partial(within_kernel, steps - 1),
        [shape((tokens, full), F32)] * 2,
        (query, keys, values, decay, *entering),
        far=4,
        scratch=[*blocks, dma((4,))],
        cost=1.0,
    )
    (mine,) = call(
        functools.partial(attend_kernel, heads),
        [shape((tokens, full + LANES), BF16)],
        (query, within, factor, theirs, norm_gain[None, :]),
    )
    mate = swap(mine, "head", 1)
    ahead = {}
    for far in range(1, far_count):
        (ahead[far],) = call(
            functools.partial(ahead_kernel, full),
            [shape((tokens, columns), F32)],
            (mine, my_weights[far]),
            cost=0.4,
        )

    received = [[[] for _ in range(PARTS)] for _ in range(far_count)]
    reach = far_count // 2
    while reach:
        for far in range(reach, 2 * reach):
            for part, (first, end) in enumerate(zip(cuts[:-1], cuts[1:])):
                (away,) = call(
                    functools.partial(away_kernel, full, first, part == PARTS - 2),
                    [shape(((end - first) * tokens + SUBLANES * (part == PARTS - 2), LANES), BF16)],
                    (ahead[far], mine, mate, their_weights[far], *received[far][part]),
                    cost=0.2,
                )
                hop = 3 if reach == 1 and part == PARTS - 1 else reach << 1
                received[far - reach][part].append(swap(away, "head", hop))
        reach //= 2
    (partial,) = call(
        functools.partial(home_kernel, full),
        [shape((tokens, columns), F32)],
        (mine, mate, my_weights[0], their_weights[0]),
        cost=0.6,
    )
    widths = [(end - first) * LANES for first, end in zip(cuts[:-1], cuts[1:])]
    scale, *done = call(
        functools.partial(middle_kernel, full, cuts[: PARTS - 1], len(received[0][0])),
        [shape((tokens, 1), F32)] + [shape((tokens, width), BF16) for width in widths[:-1]],
        (mine, mate, partial, *(other for group in received[0][:-1] for other in group)),
        cost=0.3,
    )
    (mixed,) = call(
        functools.partial(last_kernel, cuts[PARTS - 1], len(done)),
        [shape((tokens, columns), BF16)],
        (partial, scale, *done, *received[0][PARTS - 1]),
        out_places=[FAR],
        scratch=[pltpu.VMEM((tokens, widths[-1]), BF16), dma((PARTS,))],
    )
    return mixed


def solution(mesh):
    placed = (
        P("ctx", "head"),
        P("ctx", "head"),
        P("ctx", "head"),
        P("ctx", "head"),
        P("head"),
        P("head", None),
    )
    return jax.shard_map(
        local, mesh=mesh, in_specs=placed, out_specs=P("ctx", "head"), check_vma=False
    )
```

```python
import functools

import jax
import jax.numpy as jnp
from jax import lax
from jax.experimental import pallas as pl
from jax.experimental.pallas import tpu as pltpu
from jax.sharding import PartitionSpec as P

F32, BF16 = jnp.float32, jnp.bfloat16
HIGHEST = lax.Precision.HIGHEST
VMEM = pl.BlockSpec(memory_space=pltpu.VMEM)
FAR = pl.BlockSpec(memory_space=pltpu.HBM)
LANES = 128
SUBLANES = 16
PARTS = 3


def call(body, outs, operands, far=0, out_places=None, scratch=(), cost=1.0):
    held = [pltpu.with_memory_space_constraint(o, pltpu.HBM) for o in operands[:far]]
    return pl.pallas_call(
        body,
        out_shape=outs,
        in_specs=[FAR] * far + [VMEM] * (len(operands) - far),
        out_specs=out_places or [VMEM] * len(outs),
        scratch_shapes=scratch,
        cost_estimate=pl.CostEstimate(flops=int(cost * 1e9), bytes_accessed=int(cost * 1e6), transcendentals=0),
        compiler_params=pltpu.CompilerParams(vmem_limit_bytes=32 << 20),
    )(*held, *operands[far:])


def shape(dims, dtype):
    return jax.ShapeDtypeStruct(dims, dtype)


def padded(rows):
    return -(-rows // SUBLANES) * SUBLANES


def split3(value):
    high = value.astype(BF16)
    rest = value - high.astype(F32)
    mid = rest.astype(BF16)
    return high, mid, (rest - mid.astype(F32)).astype(BF16)


def stacked(value, heads):
    parts = list(split3(value))
    fill = padded(3 * heads) - 3 * heads
    if fill:
        parts.append(jnp.zeros((fill, LANES), BF16))
    return jnp.concatenate([part.astype(F32) for part in parts], axis=0).astype(BF16)


def unstacked(rows, heads):
    rows = rows.astype(F32)
    return rows[:heads] + rows[heads : 2 * heads] + rows[2 * heads : 3 * heads]


def triangle(tokens):
    row = lax.broadcasted_iota(jnp.int32, (tokens, tokens), 0)
    col = lax.broadcasted_iota(jnp.int32, (tokens, tokens), 1)
    return row, col


def column_sums(decay, after=False):
    heads, tokens = decay.shape
    row, col = triangle(tokens)
    lower = jnp.where(row < col if after else row >= col, 1.0, 0.0).astype(BF16)
    sums = [
        lax.dot_general(lower, part, (((1,), (1,)), ((), ())), preferred_element_type=F32) for part in split3(decay)
    ]
    return sums[0] + (sums[1] + sums[2])


def row_sums(decay):
    row, col = triangle(decay.shape[1])
    upper = jnp.where(row <= col, 1.0, 0.0).astype(F32)
    return jnp.dot(decay, upper, precision=HIGHEST)


def odd(axis, step=0):
    return (lax.axis_index(axis) >> step) % 2 == 1


def fetch(sources, targets, semaphores):
    copies = [
        pltpu.make_async_copy(source, target, semaphores.at[index])
        for index, (source, target) in enumerate(zip(sources, targets))
    ]
    for copy in copies:
        copy.start()
    return copies


def states_kernel(keys_far, values_far, decay_far, message, keys, values, decay, tails, semaphores):
    decay_copy, *copies = fetch((decay_far, keys_far, values_far), (decay, keys, values), semaphores)
    decay_copy.wait()
    heads, tokens = decay.shape
    width = keys.shape[1] // heads
    tail = jnp.exp(column_sums(decay[...], after=True))
    for head in range(heads):
        tails[:, head * width : (head + 1) * width] = jnp.broadcast_to(tail[:, head : head + 1], (tokens, width))
    total = jnp.sum(decay[...], axis=1, keepdims=True)
    message[heads * width :, :] = stacked(jnp.broadcast_to(jnp.exp(total), (heads, LANES)), heads)
    for copy in copies:
        copy.wait()
    for head in range(heads):
        own = slice(head * width, (head + 1) * width)
        faded = (values[:, own].astype(F32) * tails[:, own]).astype(BF16)
        state = lax.dot_general(
            keys[:, own], faded, (((0,), (0,)), ((), ())), preferred_element_type=F32
        )
        message[own, :] = state.astype(BF16)


def weights_kernel(far_count, split, weight_far, _, *refs):
    *weights, token, semaphores = refs
    columns = weights[0].shape[1]
    me = lax.axis_index("head")
    copies = []

    def copy(owner, first, end, target):
        start = pl.multiple_of(owner * columns + first, LANES)
        source = weight_far.at[:, pl.ds(start, end - first)]
        copies.append(pltpu.make_async_copy(source, target.at[:, first:end], semaphores.at[len(copies)]))
        copies[-1].start()

    for index, target in enumerate(weights):
        far = far_count - 1 - index // 2
        owner = me ^ (far << 1) ^ (1 - index % 2)
        if far % 2:
            copy(owner, 0, split, target)
            copy(owner ^ 1, split, columns, target)
        else:
            copy(owner, 0, columns, target)
    token[...] = jnp.zeros_like(token)
    for one in copies:
        one.wait()


def within_kernel(step, query_far, keys_far, values_far, decay_far, before, before_decay, *refs):
    within, factor, query, keys, values, decay, semaphores = refs
    for copy in fetch((query_far, keys_far, values_far, decay_far), (query, keys, values, decay), semaphores):
        copy.wait()
    heads, tokens = decay.shape
    width = keys.shape[1] // heads
    column = column_sums(decay[...])
    line = row_sums(decay[...])
    grown = jnp.exp(column)
    scale = jnp.where(odd("ctx", step), before_decay[...], 0.0 * before_decay[...])
    row, col = triangle(tokens)
    for head in range(heads):
        own = slice(head * width, (head + 1) * width)
        scores = lax.dot_general(
            query[:, own], keys[:, own], (((1,), (1,)), ((), ())), preferred_element_type=F32
        )
        differ = jnp.where(row >= col, column[:, head : head + 1] - line[head : head + 1, :], -1e30)
        weights = (jnp.exp(differ) * scores).astype(BF16)
        carried = jnp.dot(query[:, own], before[own, :].astype(BF16), preferred_element_type=F32)
        spread = jnp.broadcast_to(grown[:, head : head + 1], (tokens, width))
        within[:, own] = jnp.dot(weights, values[:, own], preferred_element_type=F32) + spread * carried
        factor[:, own] = spread * scale[head : head + 1]


def join_kernel(step, heads, *refs):
    first = step == 0
    if first:
        mine, theirs, _, joined, entering, entering_decay = refs
    else:
        mine, theirs, before, before_decay, joined, entering, entering_decay = refs
    later = odd("ctx", step)
    rows = mine.shape[0] - padded(3 * heads)
    width = rows // heads
    my_decay = unstacked(mine[rows:, :], heads)
    their_decay = unstacked(theirs[rows:, :], heads)
    one = jnp.ones_like(my_decay)
    for_theirs = jnp.where(later, my_decay, one)
    for_mine = jnp.where(later, one, their_decay)
    if first:
        for_entering = jnp.where(later, one, 0.0 * one)
        entering_decay[...] = jnp.where(later, their_decay, one)
    else:
        for_entering = jnp.where(later, before_decay[...], 0.0 * one)
        entering_decay[...] = before_decay[...] * jnp.where(later, their_decay, one)
    for head in range(heads):
        own = slice(head * width, (head + 1) * width)
        row = slice(head, head + 1)
        received = theirs[own, :].astype(F32)
        joined[own, :] = (for_theirs[row] * received + for_mine[row] * mine[own, :].astype(F32)).astype(BF16)
        added = for_entering[row] * received
        entering[own, :] = added if first else before[own, :] + added
    if joined.shape[0] > rows:
        joined[rows:, :] = stacked(my_decay * their_decay, heads)


def attend_kernel(heads, query, within, factor, theirs, gain, message):
    tokens, full = query.shape
    width = full // heads
    squares = jnp.zeros((tokens, width), F32)
    for head in range(heads):
        own = slice(head * width, (head + 1) * width)
        carried = jnp.dot(query[:, own], theirs[own, :], preferred_element_type=F32)
        attn = within[:, own] + factor[:, own] * carried
        squares = squares + attn * attn
        message[:, own] = (attn * gain[:, own]).astype(BF16)
    message[:, full:] = squares.astype(BF16)


def squares_row(mine, theirs, full):
    column = jnp.sum(mine[:, full:].astype(F32) + theirs[:, full:].astype(F32), axis=1, keepdims=True)
    row, col = triangle(mine.shape[0])
    return jnp.sum(jnp.where(row == col, column, 0.0), axis=0, keepdims=True)


def ahead_kernel(full, mine, weight, result):
    result[...] = jnp.dot(mine[:, :full], weight[...], preferred_element_type=F32)


def away_kernel(full, first_block, leading, partial, mine, theirs, their_weight, *refs):
    *received, message = refs
    tokens = mine.shape[0]
    blocks = message.shape[0] // tokens
    columns = slice(first_block * LANES, (first_block + blocks) * LANES)
    result = partial[:, columns] + jnp.dot(theirs[:, :full], their_weight[:, columns], preferred_element_type=F32)
    for block in range(blocks):
        there = slice(block * tokens, (block + 1) * tokens)
        part = result[:, block * LANES : (block + 1) * LANES]
        for other in received:
            part = part + other[there, :].astype(F32)
        message[there, :] = part.astype(BF16)
    if leading:
        total = squares_row(mine, theirs, full)
        for other in received:
            total = total + unstacked(other[blocks * tokens :, :], 1)
        message[blocks * tokens :, :] = stacked(total, 1)


def home_kernel(full, mine, theirs, my_weight, their_weight, result):
    result[...] = jnp.dot(mine[:, :full], my_weight[...], preferred_element_type=F32) + jnp.dot(
        theirs[:, :full], their_weight[...], preferred_element_type=F32
    )


def scaled(partial, first_block, received, scale, out):
    tokens, columns = out.shape
    for block in range(columns // LANES):
        summed = partial[:, (first_block + block) * LANES : (first_block + block + 1) * LANES]
        for other in received:
            summed = summed + other[block * tokens : (block + 1) * tokens, :].astype(F32)
        out[:, block * LANES : (block + 1) * LANES] = (summed * scale).astype(BF16)


def middle_kernel(full, cuts, count, sent, partial, *refs):
    received, (scale, *outs) = refs[: len(cuts) * count], refs[len(cuts) * count :]
    groups = [received[part * count : (part + 1) * count] for part in range(len(cuts))]
    total = unstacked(sent[sent.shape[0] - SUBLANES :, :], 1)
    for other in groups[-1]:
        total = total + unstacked(other[other.shape[0] - SUBLANES :, :], 1)
    row, col = triangle(partial.shape[0])
    total = jnp.sum(jnp.where(row == col, total, 0.0), axis=1, keepdims=True)
    factor = lax.rsqrt(total / (full * lax.axis_size("head")) + 1e-05)
    scale[...] = factor
    for first_block, group, out in zip(cuts, groups, outs):
        scaled(partial, first_block, group, factor, out)


def last_kernel(first_block, done_count, partial, scale, *refs):
    done, received = refs[:done_count], refs[done_count:-3]
    out, staged, semaphores = refs[-3:]
    copies = []

    def write(source, column):
        there = out.at[:, column : column + source.shape[1]]
        copies.append(pltpu.make_async_copy(source, there, semaphores.at[len(copies)]))
        copies[-1].start()

    column = 0
    for part in done:
        write(part, column)
        column += part.shape[1]
    scaled(partial, first_block, received, scale[...], staged)
    write(staged, column)
    for copy in copies:
        copy.wait()


def local(query, keys, values, log_decay, norm_gain, out_weight):
    tokens, full = query.shape
    heads = log_decay.shape[1]
    steps = lax.axis_size("ctx").bit_length() - 1
    groups = lax.axis_size("head")
    columns = out_weight.shape[1] // groups
    decay = log_decay.T
    message_shape = shape((full + padded(3 * heads), LANES), BF16)
    dma = pltpu.SemaphoreType.DMA

    def swap(value, axis, bit):
        count = lax.axis_size(axis)
        return lax.ppermute(value, axis, [(i, i ^ bit) for i in range(count)])

    blocks = [pltpu.VMEM(array.shape, array.dtype) for array in (query, keys, values, decay)]
    (message,) = call(
        states_kernel,
        [message_shape],
        (keys, values, decay),
        far=3,
        scratch=[*blocks[1:], pltpu.VMEM((tokens, full), F32), dma((3,))],
    )
    theirs = swap(message, "ctx", 1)

    far_count = groups // 2
    blocks_out = columns // LANES
    cuts = [0, blocks_out // 3, blocks_out - blocks_out // 4, blocks_out]
    *weights, token = call(
        functools.partial(weights_kernel, far_count, cuts[-2] * LANES),
        [shape((full, columns), BF16)] * (2 * far_count) + [shape((8, LANES), F32)],
        (out_weight, message),
        far=1,
        scratch=[dma((3 * far_count,))],
        cost=2.0,
    )
    my_weights, their_weights = {}, {}
    for index in range(0, 2 * far_count, 2):
        far = far_count - 1 - index // 2
        their_weights[far] = swap(weights[index], "head", 1)
        my_weights[far] = weights[index + 1]

    entering = (token,)
    for step in range(steps - 1):
        message, *entering = call(
            functools.partial(join_kernel, step, heads),
            [
                message_shape if step < steps - 2 else shape((full, LANES), BF16),
                shape((full, LANES), F32),
                shape((heads, LANES), F32),
            ],
            (message, theirs, *entering),
            cost=30.0 if step == steps - 2 else 0.1,
        )
        theirs = swap(message, "ctx", 2 << step)
    within, factor = call(
        functools.partial(within_kernel, steps - 1),
        [shape((tokens, full), F32)] * 2,
        (query, keys, values, decay, *entering),
        far=4,
        scratch=[*blocks, dma((4,))],
        cost=1.0,
    )
    (mine,) = call(
        functools.partial(attend_kernel, heads),
        [shape((tokens, full + LANES), BF16)],
        (query, within, factor, theirs, norm_gain[None, :]),
    )
    mate = swap(mine, "head", 1)
    ahead = {}
    for far in range(1, far_count):
        (ahead[far],) = call(
            functools.partial(ahead_kernel, full),
            [shape((tokens, columns), F32)],
            (mine, my_weights[far]),
            cost=0.4,
        )

    received = [[[] for _ in range(PARTS)] for _ in range(far_count)]
    reach = far_count // 2
    sent = None
    while reach:
        for far in range(reach, 2 * reach):
            for part, (first, end) in enumerate(zip(cuts[:-1], cuts[1:])):
                (away,) = call(
                    functools.partial(away_kernel, full, first, part == PARTS - 2),
                    [shape(((end - first) * tokens + SUBLANES * (part == PARTS - 2), LANES), BF16)],
                    (ahead[far], mine, mate, their_weights[far], *received[far][part]),
                    cost=0.2,
                )
                if part == PARTS - 2 and sent is None:
                    sent = away
                hop = 3 if reach == 1 and part == PARTS - 1 else reach << 1
                received[far - reach][part].append(swap(away, "head", hop))
        reach //= 2
    (partial,) = call(
        functools.partial(home_kernel, full),
        [shape((tokens, columns), F32)],
        (mine, mate, my_weights[0], their_weights[0]),
        cost=0.6,
    )
    widths = [(end - first) * LANES for first, end in zip(cuts[:-1], cuts[1:])]
    scale, *done = call(
        functools.partial(middle_kernel, full, cuts[: PARTS - 1], len(received[0][0])),
        [shape((tokens, 1), F32)] + [shape((tokens, width), BF16) for width in widths[:-1]],
        (sent, partial, *(other for group in received[0][:-1] for other in group)),
        cost=0.3,
    )
    (mixed,) = call(
        functools.partial(last_kernel, cuts[PARTS - 1], len(done)),
        [shape((tokens, columns), BF16)],
        (partial, scale, *done, *received[0][PARTS - 1]),
        out_places=[FAR],
        scratch=[pltpu.VMEM((tokens, widths[-1]), BF16), dma((PARTS,))],
    )
    return mixed


def solution(mesh):
    placed = (
        P("ctx", "head"),
        P("ctx", "head"),
        P("ctx", "head"),
        P("ctx", "head"),
        P("head"),
        P("head", None),
    )
    return jax.shard_map(
        local, mesh=mesh, in_specs=placed, out_specs=P("ctx", "head"), check_vma=False
    )
```

```python
import functools

import jax
import jax.numpy as jnp
from jax import lax
from jax.experimental import pallas as pl
from jax.experimental.pallas import tpu as pltpu
from jax.sharding import PartitionSpec as P

F32, BF16 = jnp.float32, jnp.bfloat16
HIGHEST = lax.Precision.HIGHEST
VMEM = pl.BlockSpec(memory_space=pltpu.VMEM)
FAR = pl.BlockSpec(memory_space=pltpu.HBM)
LANES = 128
SUBLANES = 16
PARTS = 3


def call(body, outs, operands, far=0, out_places=None, scratch=(), cost=1.0):
    held = [pltpu.with_memory_space_constraint(o, pltpu.HBM) for o in operands[:far]]
    return pl.pallas_call(
        body,
        out_shape=outs,
        in_specs=[FAR] * far + [VMEM] * (len(operands) - far),
        out_specs=out_places or [VMEM] * len(outs),
        scratch_shapes=scratch,
        cost_estimate=pl.CostEstimate(flops=int(cost * 1e9), bytes_accessed=int(cost * 1e6), transcendentals=0),
        compiler_params=pltpu.CompilerParams(vmem_limit_bytes=32 << 20),
    )(*held, *operands[far:])


def shape(dims, dtype):
    return jax.ShapeDtypeStruct(dims, dtype)


def padded(rows):
    return -(-rows // SUBLANES) * SUBLANES


def split3(value):
    high = value.astype(BF16)
    rest = value - high.astype(F32)
    mid = rest.astype(BF16)
    return high, mid, (rest - mid.astype(F32)).astype(BF16)


def stacked(value, heads):
    parts = list(split3(value))
    fill = padded(3 * heads) - 3 * heads
    if fill:
        parts.append(jnp.zeros((fill, LANES), BF16))
    return jnp.concatenate([part.astype(F32) for part in parts], axis=0).astype(BF16)


def unstacked(rows, heads):
    rows = rows.astype(F32)
    return rows[:heads] + rows[heads : 2 * heads] + rows[2 * heads : 3 * heads]


def triangle(tokens):
    row = lax.broadcasted_iota(jnp.int32, (tokens, tokens), 0)
    col = lax.broadcasted_iota(jnp.int32, (tokens, tokens), 1)
    return row, col


def column_sums(decay):
    heads, tokens = decay.shape
    row, col = triangle(tokens)
    lower = jnp.where(row >= col, 1.0, 0.0).astype(BF16)
    sums = [
        lax.dot_general(lower, part, (((1,), (1,)), ((), ())), preferred_element_type=F32) for part in split3(decay)
    ]
    return sums[0] + (sums[1] + sums[2])


def row_sums(decay):
    row, col = triangle(decay.shape[1])
    upper = jnp.where(row <= col, 1.0, 0.0).astype(F32)
    return jnp.dot(decay, upper, precision=HIGHEST)


def odd(axis, step=0):
    return (lax.axis_index(axis) >> step) % 2 == 1


def fetch(sources, targets, semaphores):
    copies = [
        pltpu.make_async_copy(source, target, semaphores.at[index])
        for index, (source, target) in enumerate(zip(sources, targets))
    ]
    for copy in copies:
        copy.start()
    return copies


def states_kernel(keys_far, values_far, decay_far, message, keys, values, decay, tails, semaphores):
    decay_copy, *copies = fetch((decay_far, keys_far, values_far), (decay, keys, values), semaphores)
    decay_copy.wait()
    heads, tokens = decay.shape
    width = keys.shape[1] // heads
    column = column_sums(decay[...])
    tail = jnp.exp(column[tokens - 1 : tokens, :] - column)
    for head in range(heads):
        tails[:, head * width : (head + 1) * width] = jnp.broadcast_to(tail[:, head : head + 1], (tokens, width))
    total = jnp.sum(decay[...], axis=1, keepdims=True)
    message[heads * width :, :] = stacked(jnp.broadcast_to(jnp.exp(total), (heads, LANES)), heads)
    for copy in copies:
        copy.wait()
    for head in range(heads):
        own = slice(head * width, (head + 1) * width)
        faded = (values[:, own].astype(F32) * tails[:, own]).astype(BF16)
        state = lax.dot_general(
            keys[:, own], faded, (((0,), (0,)), ((), ())), preferred_element_type=F32
        )
        message[own, :] = state.astype(BF16)


def weights_kernel(far_count, split, weight_far, _, *refs):
    *weights, token, semaphores = refs
    columns = weights[0].shape[1]
    me = lax.axis_index("head")
    copies = []

    def copy(owner, first, end, target):
        start = pl.multiple_of(owner * columns + first, LANES)
        source = weight_far.at[:, pl.ds(start, end - first)]
        copies.append(pltpu.make_async_copy(source, target.at[:, first:end], semaphores.at[len(copies)]))
        copies[-1].start()

    for index, target in enumerate(weights):
        far = far_count - 1 - index // 2
        owner = me ^ (far << 1) ^ (1 - index % 2)
        if far % 2:
            copy(owner, 0, split, target)
            copy(owner ^ 1, split, columns, target)
        else:
            copy(owner, 0, columns, target)
    token[...] = jnp.zeros_like(token)
    for one in copies:
        one.wait()


def within_kernel(step, query_far, keys_far, values_far, decay_far, before, before_decay, *refs):
    within, factor, query, keys, values, decay, semaphores = refs
    for copy in fetch((query_far, keys_far, values_far, decay_far), (query, keys, values, decay), semaphores):
        copy.wait()
    heads, tokens = decay.shape
    width = keys.shape[1] // heads
    column = column_sums(decay[...])
    line = row_sums(decay[...])
    grown = jnp.exp(column)
    scale = jnp.where(odd("ctx", step), before_decay[...], 0.0 * before_decay[...])
    row, col = triangle(tokens)
    for head in range(heads):
        own = slice(head * width, (head + 1) * width)
        scores = lax.dot_general(
            query[:, own], keys[:, own], (((1,), (1,)), ((), ())), preferred_element_type=F32
        )
        differ = jnp.where(row >= col, column[:, head : head + 1] - line[head : head + 1, :], -1e30)
        weights = (jnp.exp(differ) * scores).astype(BF16)
        carried = jnp.dot(query[:, own], before[own, :].astype(BF16), preferred_element_type=F32)
        spread = jnp.broadcast_to(grown[:, head : head + 1], (tokens, width))
        within[:, own] = jnp.dot(weights, values[:, own], preferred_element_type=F32) + spread * carried
        factor[:, own] = spread * scale[head : head + 1]


def join_kernel(step, heads, *refs):
    first = step == 0
    if first:
        mine, theirs, _, joined, entering, entering_decay = refs
    else:
        mine, theirs, before, before_decay, joined, entering, entering_decay = refs
    later = odd("ctx", step)
    rows = mine.shape[0] - padded(3 * heads)
    width = rows // heads
    my_decay = unstacked(mine[rows:, :], heads)
    their_decay = unstacked(theirs[rows:, :], heads)
    one = jnp.ones_like(my_decay)
    for_theirs = jnp.where(later, my_decay, one)
    for_mine = jnp.where(later, one, their_decay)
    if first:
        for_entering = jnp.where(later, one, 0.0 * one)
        entering_decay[...] = jnp.where(later, their_decay, one)
    else:
        for_entering = jnp.where(later, before_decay[...], 0.0 * one)
        entering_decay[...] = before_decay[...] * jnp.where(later, their_decay, one)
    for head in range(heads):
        own = slice(head * width, (head + 1) * width)
        row = slice(head, head + 1)
        received = theirs[own, :].astype(F32)
        joined[own, :] = (for_theirs[row] * received + for_mine[row] * mine[own, :].astype(F32)).astype(BF16)
        added = for_entering[row] * received
        entering[own, :] = added if first else before[own, :] + added
    if joined.shape[0] > rows:
        joined[rows:, :] = stacked(my_decay * their_decay, heads)


def attend_kernel(heads, query, within, factor, theirs, gain, message):
    tokens, full = query.shape
    width = full // heads
    squares = jnp.zeros((tokens, width), F32)
    for head in range(heads):
        own = slice(head * width, (head + 1) * width)
        carried = jnp.dot(query[:, own], theirs[own, :], preferred_element_type=F32)
        attn = within[:, own] + factor[:, own] * carried
        squares = squares + attn * attn
        message[:, own] = (attn * gain[:, own]).astype(BF16)
    message[:, full:] = squares.astype(BF16)


def squares_row(mine, theirs, full):
    column = jnp.sum(mine[:, full:].astype(F32) + theirs[:, full:].astype(F32), axis=1, keepdims=True)
    row, col = triangle(mine.shape[0])
    return jnp.sum(jnp.where(row == col, column, 0.0), axis=0, keepdims=True)


def ahead_kernel(full, mine, weight, result):
    result[...] = jnp.dot(mine[:, :full], weight[...], preferred_element_type=F32)


def away_kernel(full, first_block, leading, partial, mine, theirs, their_weight, *refs):
    *received, message = refs
    tokens = mine.shape[0]
    blocks = message.shape[0] // tokens
    columns = slice(first_block * LANES, (first_block + blocks) * LANES)
    result = partial[:, columns] + jnp.dot(theirs[:, :full], their_weight[:, columns], preferred_element_type=F32)
    for block in range(blocks):
        there = slice(block * tokens, (block + 1) * tokens)
        part = result[:, block * LANES : (block + 1) * LANES]
        for other in received:
            part = part + other[there, :].astype(F32)
        message[there, :] = part.astype(BF16)
    if leading:
        total = squares_row(mine, theirs, full)
        for other in received:
            total = total + unstacked(other[blocks * tokens :, :], 1)
        message[blocks * tokens :, :] = stacked(total, 1)


def home_kernel(full, mine, theirs, my_weight, their_weight, result):
    result[...] = jnp.dot(mine[:, :full], my_weight[...], preferred_element_type=F32) + jnp.dot(
        theirs[:, :full], their_weight[...], preferred_element_type=F32
    )


def scaled(partial, first_block, received, scale, out):
    tokens, columns = out.shape
    for block in range(columns // LANES):
        summed = partial[:, (first_block + block) * LANES : (first_block + block + 1) * LANES]
        for other in received:
            summed = summed + other[block * tokens : (block + 1) * tokens, :].astype(F32)
        out[:, block * LANES : (block + 1) * LANES] = (summed * scale).astype(BF16)


def middle_kernel(full, cuts, count, mine, theirs, partial, *refs):
    received, (scale, *outs) = refs[: len(cuts) * count], refs[len(cuts) * count :]
    groups = [received[part * count : (part + 1) * count] for part in range(len(cuts))]
    total = squares_row(mine, theirs, full)
    for other in groups[-1]:
        total = total + unstacked(other[other.shape[0] - SUBLANES :, :], 1)
    row, col = triangle(mine.shape[0])
    total = jnp.sum(jnp.where(row == col, total, 0.0), axis=1, keepdims=True)
    factor = lax.rsqrt(total / (full * lax.axis_size("head")) + 1e-05)
    scale[...] = factor
    for first_block, group, out in zip(cuts, groups, outs):
        scaled(partial, first_block, group, factor, out)


def last_kernel(first_block, done_count, partial, scale, *refs):
    done, received = refs[:done_count], refs[done_count:-3]
    out, staged, semaphores = refs[-3:]
    copies = []

    def write(source, column):
        there = out.at[:, column : column + source.shape[1]]
        copies.append(pltpu.make_async_copy(source, there, semaphores.at[len(copies)]))
        copies[-1].start()

    column = 0
    for part in done:
        write(part, column)
        column += part.shape[1]
    scaled(partial, first_block, received, scale[...], staged)
    write(staged, column)
    for copy in copies:
        copy.wait()


def local(query, keys, values, log_decay, norm_gain, out_weight):
    tokens, full = query.shape
    heads = log_decay.shape[1]
    steps = lax.axis_size("ctx").bit_length() - 1
    groups = lax.axis_size("head")
    columns = out_weight.shape[1] // groups
    decay = log_decay.T
    message_shape = shape((full + padded(3 * heads), LANES), BF16)
    dma = pltpu.SemaphoreType.DMA

    def swap(value, axis, bit):
        count = lax.axis_size(axis)
        return lax.ppermute(value, axis, [(i, i ^ bit) for i in range(count)])

    blocks = [pltpu.VMEM(array.shape, array.dtype) for array in (query, keys, values, decay)]
    (message,) = call(
        states_kernel,
        [message_shape],
        (keys, values, decay),
        far=3,
        scratch=[*blocks[1:], pltpu.VMEM((tokens, full), F32), dma((3,))],
    )
    theirs = swap(message, "ctx", 1)

    far_count = groups // 2
    blocks_out = columns // LANES
    cuts = [0, blocks_out * 5 // 12, blocks_out - blocks_out // 4, blocks_out]
    *weights, token = call(
        functools.partial(weights_kernel, far_count, cuts[-2] * LANES),
        [shape((full, columns), BF16)] * (2 * far_count) + [shape((8, LANES), F32)],
        (out_weight, message),
        far=1,
        scratch=[dma((3 * far_count,))],
        cost=2.0,
    )
    my_weights, their_weights = {}, {}
    for index in range(0, 2 * far_count, 2):
        far = far_count - 1 - index // 2
        their_weights[far] = swap(weights[index], "head", 1)
        my_weights[far] = weights[index + 1]

    entering = (token,)
    for step in range(steps - 1):
        message, *entering = call(
            functools.partial(join_kernel, step, heads),
            [
                message_shape if step < steps - 2 else shape((full, LANES), BF16),
                shape((full, LANES), F32),
                shape((heads, LANES), F32),
            ],
            (message, theirs, *entering),
            cost=30.0 if step == steps - 2 else 0.1,
        )
        theirs = swap(message, "ctx", 2 << step)
    within, factor = call(
        functools.partial(within_kernel, steps - 1),
        [shape((tokens, full), F32)] * 2,
        (query, keys, values, decay, *entering),
        far=4,
        scratch=[*blocks, dma((4,))],
        cost=1.0,
    )
    (mine,) = call(
        functools.partial(attend_kernel, heads),
        [shape((tokens, full + LANES), BF16)],
        (query, within, factor, theirs, norm_gain[None, :]),
    )
    mate = swap(mine, "head", 1)
    ahead = {}
    for far in range(1, far_count):
        (ahead[far],) = call(
            functools.partial(ahead_kernel, full),
            [shape((tokens, columns), F32)],
            (mine, my_weights[far]),
            cost=0.4,
        )

    received = [[[] for _ in range(PARTS)] for _ in range(far_count)]
    reach = far_count // 2
    while reach:
        for far in range(reach, 2 * reach):
            for part, (first, end) in enumerate(zip(cuts[:-1], cuts[1:])):
                (away,) = call(
                    functools.partial(away_kernel, full, first, part == PARTS - 2),
                    [shape(((end - first) * tokens + SUBLANES * (part == PARTS - 2), LANES), BF16)],
                    (ahead[far], mine, mate, their_weights[far], *received[far][part]),
                    cost=0.2,
                )
                hop = 3 if reach == 1 and part == PARTS - 1 else reach << 1
                received[far - reach][part].append(swap(away, "head", hop))
        reach //= 2
    (partial,) = call(
        functools.partial(home_kernel, full),
        [shape((tokens, columns), F32)],
        (mine, mate, my_weights[0], their_weights[0]),
        cost=0.6,
    )
    widths = [(end - first) * LANES for first, end in zip(cuts[:-1], cuts[1:])]
    scale, *done = call(
        functools.partial(middle_kernel, full, cuts[: PARTS - 1], len(received[0][0])),
        [shape((tokens, 1), F32)] + [shape((tokens, width), BF16) for width in widths[:-1]],
        (mine, mate, partial, *(other for group in received[0][:-1] for other in group)),
        cost=0.3,
    )
    (mixed,) = call(
        functools.partial(last_kernel, cuts[PARTS - 1], len(done)),
        [shape((tokens, columns), BF16)],
        (partial, scale, *done, *received[0][PARTS - 1]),
        out_places=[FAR],
        scratch=[pltpu.VMEM((tokens, widths[-1]), BF16), dma((PARTS,))],
    )
    return mixed


def solution(mesh):
    placed = (
        P("ctx", "head"),
        P("ctx", "head"),
        P("ctx", "head"),
        P("ctx", "head"),
        P("head"),
        P("head", None),
    )
    return jax.shard_map(
        local, mesh=mesh, in_specs=placed, out_specs=P("ctx", "head"), check_vma=False
    )
```

```python
import functools

import jax
import jax.numpy as jnp
from jax import lax
from jax.experimental import pallas as pl
from jax.experimental.pallas import tpu as pltpu
from jax.sharding import PartitionSpec as P

F32, BF16 = jnp.float32, jnp.bfloat16
HIGHEST = lax.Precision.HIGHEST
VMEM = pl.BlockSpec(memory_space=pltpu.VMEM)
FAR = pl.BlockSpec(memory_space=pltpu.HBM)
LANES = 128
SUBLANES = 16
PARTS = 3


def call(body, outs, operands, far=0, out_places=None, scratch=(), cost=1.0):
    held = [pltpu.with_memory_space_constraint(o, pltpu.HBM) for o in operands[:far]]
    return pl.pallas_call(
        body,
        out_shape=outs,
        in_specs=[FAR] * far + [VMEM] * (len(operands) - far),
        out_specs=out_places or [VMEM] * len(outs),
        scratch_shapes=scratch,
        cost_estimate=pl.CostEstimate(flops=int(cost * 1e9), bytes_accessed=int(cost * 1e6), transcendentals=0),
        compiler_params=pltpu.CompilerParams(vmem_limit_bytes=32 << 20),
    )(*held, *operands[far:])


def shape(dims, dtype):
    return jax.ShapeDtypeStruct(dims, dtype)


def padded(rows):
    return -(-rows // SUBLANES) * SUBLANES


def split3(value):
    high = value.astype(BF16)
    rest = value - high.astype(F32)
    mid = rest.astype(BF16)
    return high, mid, (rest - mid.astype(F32)).astype(BF16)


def stacked(value, heads):
    parts = list(split3(value))
    fill = padded(3 * heads) - 3 * heads
    if fill:
        parts.append(jnp.zeros((fill, LANES), BF16))
    return jnp.concatenate([part.astype(F32) for part in parts], axis=0).astype(BF16)


def unstacked(rows, heads):
    rows = rows.astype(F32)
    return rows[:heads] + rows[heads : 2 * heads] + rows[2 * heads : 3 * heads]


def triangle(tokens):
    row = lax.broadcasted_iota(jnp.int32, (tokens, tokens), 0)
    col = lax.broadcasted_iota(jnp.int32, (tokens, tokens), 1)
    return row, col


def column_sums(decay):
    heads, tokens = decay.shape
    row, col = triangle(tokens)
    lower = jnp.where(row >= col, 1.0, 0.0).astype(BF16)
    sums = [
        lax.dot_general(lower, part, (((1,), (1,)), ((), ())), preferred_element_type=F32) for part in split3(decay)
    ]
    return sums[0] + (sums[1] + sums[2])


def row_sums(decay):
    row, col = triangle(decay.shape[1])
    upper = jnp.where(row <= col, 1.0, 0.0).astype(F32)
    return jnp.dot(decay, upper, precision=HIGHEST)


def odd(axis, step=0):
    return (lax.axis_index(axis) >> step) % 2 == 1


def fetch(sources, targets, semaphores):
    copies = [
        pltpu.make_async_copy(source, target, semaphores.at[index])
        for index, (source, target) in enumerate(zip(sources, targets))
    ]
    for copy in copies:
        copy.start()
    return copies


def states_kernel(keys_far, values_far, decay_far, message, keys, values, decay, tails, semaphores):
    decay_copy, *copies = fetch((decay_far, keys_far, values_far), (decay, keys, values), semaphores)
    decay_copy.wait()
    heads, tokens = decay.shape
    width = keys.shape[1] // heads
    column = column_sums(decay[...])
    tail = jnp.exp(column[tokens - 1 : tokens, :] - column)
    for head in range(heads):
        tails[:, head * width : (head + 1) * width] = jnp.broadcast_to(tail[:, head : head + 1], (tokens, width))
    total = jnp.sum(decay[...], axis=1, keepdims=True)
    message[heads * width :, :] = stacked(jnp.broadcast_to(jnp.exp(total), (heads, LANES)), heads)
    for copy in copies:
        copy.wait()
    for head in range(heads):
        own = slice(head * width, (head + 1) * width)
        faded = (values[:, own].astype(F32) * tails[:, own]).astype(BF16)
        state = lax.dot_general(
            keys[:, own], faded, (((0,), (0,)), ((), ())), preferred_element_type=F32
        )
        message[own, :] = state.astype(BF16)


def weights_kernel(far_count, split, weight_far, _, *refs):
    *weights, token, semaphores = refs
    columns = weights[0].shape[1]
    me = lax.axis_index("head")
    copies = []

    def copy(owner, first, end, target):
        start = pl.multiple_of(owner * columns + first, LANES)
        source = weight_far.at[:, pl.ds(start, end - first)]
        copies.append(pltpu.make_async_copy(source, target.at[:, first:end], semaphores.at[len(copies)]))
        copies[-1].start()

    for index, target in enumerate(weights):
        far = far_count - 1 - index // 2
        owner = me ^ (far << 1) ^ (1 - index % 2)
        if far % 2:
            copy(owner, 0, split, target)
            copy(owner ^ 1, split, columns, target)
        else:
            copy(owner, 0, columns, target)
    token[...] = jnp.zeros_like(token)
    for one in copies:
        one.wait()


def within_kernel(step, query_far, keys_far, values_far, decay_far, before, before_decay, *refs):
    within, factor, query, keys, values, decay, semaphores = refs
    for copy in fetch((query_far, keys_far, values_far, decay_far), (query, keys, values, decay), semaphores):
        copy.wait()
    heads, tokens = decay.shape
    width = keys.shape[1] // heads
    column = column_sums(decay[...])
    line = row_sums(decay[...])
    grown = jnp.exp(column)
    scale = jnp.where(odd("ctx", step), before_decay[...], 0.0 * before_decay[...])
    row, col = triangle(tokens)
    for head in range(heads):
        own = slice(head * width, (head + 1) * width)
        scores = lax.dot_general(
            query[:, own], keys[:, own], (((1,), (1,)), ((), ())), preferred_element_type=F32
        )
        differ = jnp.where(row >= col, column[:, head : head + 1] - line[head : head + 1, :], -1e30)
        weights = (jnp.exp(differ) * scores).astype(BF16)
        carried = jnp.dot(query[:, own], before[own, :].astype(BF16), preferred_element_type=F32)
        spread = jnp.broadcast_to(grown[:, head : head + 1], (tokens, width))
        within[:, own] = jnp.dot(weights, values[:, own], preferred_element_type=F32) + spread * carried
        factor[:, own] = spread * scale[head : head + 1]


def join_kernel(step, heads, *refs):
    first = step == 0
    if first:
        mine, theirs, _, joined, entering, entering_decay = refs
    else:
        mine, theirs, before, before_decay, joined, entering, entering_decay = refs
    later = odd("ctx", step)
    rows = mine.shape[0] - padded(3 * heads)
    width = rows // heads
    my_decay = unstacked(mine[rows:, :], heads)
    their_decay = unstacked(theirs[rows:, :], heads)
    one = jnp.ones_like(my_decay)
    for_theirs = jnp.where(later, my_decay, one)
    for_mine = jnp.where(later, one, their_decay)
    if first:
        for_entering = jnp.where(later, one, 0.0 * one)
        entering_decay[...] = jnp.where(later, their_decay, one)
    else:
        for_entering = jnp.where(later, before_decay[...], 0.0 * one)
        entering_decay[...] = before_decay[...] * jnp.where(later, their_decay, one)
    for head in range(heads):
        own = slice(head * width, (head + 1) * width)
        row = slice(head, head + 1)
        received = theirs[own, :].astype(F32)
        joined[own, :] = (for_theirs[row] * received + for_mine[row] * mine[own, :].astype(F32)).astype(BF16)
        added = for_entering[row] * received
        entering[own, :] = added if first else before[own, :] + added
    if joined.shape[0] > rows:
        joined[rows:, :] = stacked(my_decay * their_decay, heads)


def attend_kernel(heads, query, within, factor, theirs, gain, message):
    tokens, full = query.shape
    width = full // heads
    squares = jnp.zeros((tokens, width), F32)
    for head in range(heads):
        own = slice(head * width, (head + 1) * width)
        carried = jnp.dot(query[:, own], theirs[own, :], preferred_element_type=F32)
        attn = within[:, own] + factor[:, own] * carried
        squares = squares + attn * attn
        message[:, own] = (attn * gain[:, own]).astype(BF16)
    message[:, full:] = squares.astype(BF16)


def squares_row(mine, theirs, full):
    column = jnp.sum(mine[:, full:].astype(F32) + theirs[:, full:].astype(F32), axis=1, keepdims=True)
    row, col = triangle(mine.shape[0])
    return jnp.sum(jnp.where(row == col, column, 0.0), axis=0, keepdims=True)


def ahead_kernel(full, mine, weight, result):
    result[...] = jnp.dot(mine[:, :full], weight[...], preferred_element_type=F32)


def away_kernel(full, first_block, leading, partial, mine, theirs, their_weight, *refs):
    *received, message = refs
    tokens = mine.shape[0]
    blocks = message.shape[0] // tokens
    columns = slice(first_block * LANES, (first_block + blocks) * LANES)
    result = partial[:, columns] + jnp.dot(theirs[:, :full], their_weight[:, columns], preferred_element_type=F32)
    for block in range(blocks):
        there = slice(block * tokens, (block + 1) * tokens)
        part = result[:, block * LANES : (block + 1) * LANES]
        for other in received:
            part = part + other[there, :].astype(F32)
        message[there, :] = part.astype(BF16)
    if leading:
        total = squares_row(mine, theirs, full)
        for other in received:
            total = total + unstacked(other[blocks * tokens :, :], 1)
        message[blocks * tokens :, :] = stacked(total, 1)


def home_kernel(full, mine, theirs, my_weight, their_weight, result):
    result[...] = jnp.dot(mine[:, :full], my_weight[...], preferred_element_type=F32) + jnp.dot(
        theirs[:, :full], their_weight[...], preferred_element_type=F32
    )


def scaled(partial, first_block, received, scale, out):
    tokens, columns = out.shape
    for block in range(columns // LANES):
        summed = partial[:, (first_block + block) * LANES : (first_block + block + 1) * LANES]
        for other in received:
            summed = summed + other[block * tokens : (block + 1) * tokens, :].astype(F32)
        out[:, block * LANES : (block + 1) * LANES] = (summed * scale).astype(BF16)


def middle_kernel(full, cuts, count, mine, theirs, partial, *refs):
    received, (scale, *outs) = refs[: len(cuts) * count], refs[len(cuts) * count :]
    groups = [received[part * count : (part + 1) * count] for part in range(len(cuts))]
    total = squares_row(mine, theirs, full)
    for other in groups[-1]:
        total = total + unstacked(other[other.shape[0] - SUBLANES :, :], 1)
    row, col = triangle(mine.shape[0])
    total = jnp.sum(jnp.where(row == col, total, 0.0), axis=1, keepdims=True)
    factor = lax.rsqrt(total / (full * lax.axis_size("head")) + 1e-05)
    scale[...] = factor
    for first_block, group, out in zip(cuts, groups, outs):
        scaled(partial, first_block, group, factor, out)


def last_kernel(first_block, done_count, partial, scale, *refs):
    done, received = refs[:done_count], refs[done_count:-3]
    out, staged, semaphores = refs[-3:]
    copies = []

    def write(source, column):
        there = out.at[:, column : column + source.shape[1]]
        copies.append(pltpu.make_async_copy(source, there, semaphores.at[len(copies)]))
        copies[-1].start()

    column = 0
    for part in done:
        write(part, column)
        column += part.shape[1]
    scaled(partial, first_block, received, scale[...], staged)
    write(staged, column)
    for copy in copies:
        copy.wait()


def local(query, keys, values, log_decay, norm_gain, out_weight):
    tokens, full = query.shape
    heads = log_decay.shape[1]
    steps = lax.axis_size("ctx").bit_length() - 1
    groups = lax.axis_size("head")
    columns = out_weight.shape[1] // groups
    decay = log_decay.T
    message_shape = shape((full + padded(3 * heads), LANES), BF16)
    dma = pltpu.SemaphoreType.DMA

    def swap(value, axis, bit):
        count = lax.axis_size(axis)
        return lax.ppermute(value, axis, [(i, i ^ bit) for i in range(count)])

    blocks = [pltpu.VMEM(array.shape, array.dtype) for array in (query, keys, values, decay)]
    (message,) = call(
        states_kernel,
        [message_shape],
        (keys, values, decay),
        far=3,
        scratch=[*blocks[1:], pltpu.VMEM((tokens, full), F32), dma((3,))],
    )
    theirs = swap(message, "ctx", 1)

    far_count = groups // 2
    blocks_out = columns // LANES
    cuts = [0, blocks_out // 2, blocks_out - blocks_out // 4, blocks_out]
    *weights, token = call(
        functools.partial(weights_kernel, far_count, cuts[-2] * LANES),
        [shape((full, columns), BF16)] * (2 * far_count) + [shape((8, LANES), F32)],
        (out_weight, message),
        far=1,
        scratch=[dma((3 * far_count,))],
        cost=2.0,
    )
    my_weights, their_weights = {}, {}
    for index in range(0, 2 * far_count, 2):
        far = far_count - 1 - index // 2
        their_weights[far] = swap(weights[index], "head", 1)
        my_weights[far] = weights[index + 1]

    entering = (token,)
    for step in range(steps - 1):
        message, *entering = call(
            functools.partial(join_kernel, step, heads),
            [
                message_shape if step < steps - 2 else shape((full, LANES), BF16),
                shape((full, LANES), F32),
                shape((heads, LANES), F32),
            ],
            (message, theirs, *entering),
            cost=30.0 if step == steps - 2 else 0.1,
        )
        theirs = swap(message, "ctx", 2 << step)
    within, factor = call(
        functools.partial(within_kernel, steps - 1),
        [shape((tokens, full), F32)] * 2,
        (query, keys, values, decay, *entering),
        far=4,
        scratch=[*blocks, dma((4,))],
        cost=1.0,
    )
    (mine,) = call(
        functools.partial(attend_kernel, heads),
        [shape((tokens, full + LANES), BF16)],
        (query, within, factor, theirs, norm_gain[None, :]),
    )
    mate = swap(mine, "head", 1)
    ahead = {}
    for far in range(1, far_count):
        (ahead[far],) = call(
            functools.partial(ahead_kernel, full),
            [shape((tokens, columns), F32)],
            (mine, my_weights[far]),
            cost=0.4,
        )

    received = [[[] for _ in range(PARTS)] for _ in range(far_count)]
    reach = far_count // 2
    while reach:
        for far in range(reach, 2 * reach):
            for part, (first, end) in enumerate(zip(cuts[:-1], cuts[1:])):
                (away,) = call(
                    functools.partial(away_kernel, full, first, part == PARTS - 2),
                    [shape(((end - first) * tokens + SUBLANES * (part == PARTS - 2), LANES), BF16)],
                    (ahead[far], mine, mate, their_weights[far], *received[far][part]),
                    cost=0.2,
                )
                hop = 3 if reach == 1 and part == PARTS - 1 else reach << 1
                received[far - reach][part].append(swap(away, "head", hop))
        reach //= 2
    (partial,) = call(
        functools.partial(home_kernel, full),
        [shape((tokens, columns), F32)],
        (mine, mate, my_weights[0], their_weights[0]),
        cost=0.6,
    )
    widths = [(end - first) * LANES for first, end in zip(cuts[:-1], cuts[1:])]
    scale, *done = call(
        functools.partial(middle_kernel, full, cuts[: PARTS - 1], len(received[0][0])),
        [shape((tokens, 1), F32)] + [shape((tokens, width), BF16) for width in widths[:-1]],
        (mine, mate, partial, *(other for group in received[0][:-1] for other in group)),
        cost=0.3,
    )
    (mixed,) = call(
        functools.partial(last_kernel, cuts[PARTS - 1], len(done)),
        [shape((tokens, columns), BF16)],
        (partial, scale, *done, *received[0][PARTS - 1]),
        out_places=[FAR],
        scratch=[pltpu.VMEM((tokens, widths[-1]), BF16), dma((PARTS,))],
    )
    return mixed


def solution(mesh):
    placed = (
        P("ctx", "head"),
        P("ctx", "head"),
        P("ctx", "head"),
        P("ctx", "head"),
        P("head"),
        P("head", None),
    )
    return jax.shard_map(
        local, mesh=mesh, in_specs=placed, out_specs=P("ctx", "head"), check_vma=False
    )
```

```python
import functools

import jax
import jax.numpy as jnp
from jax import lax
from jax.experimental import pallas as pl
from jax.experimental.pallas import tpu as pltpu
from jax.sharding import PartitionSpec as P

F32, BF16 = jnp.float32, jnp.bfloat16
HIGHEST = lax.Precision.HIGHEST
VMEM = pl.BlockSpec(memory_space=pltpu.VMEM)
FAR = pl.BlockSpec(memory_space=pltpu.HBM)
LANES = 128
SUBLANES = 16
PARTS = 3


def call(body, outs, operands, far=0, out_places=None, scratch=(), cost=1.0):
    held = [pltpu.with_memory_space_constraint(o, pltpu.HBM) for o in operands[:far]]
    return pl.pallas_call(
        body,
        out_shape=outs,
        in_specs=[FAR] * far + [VMEM] * (len(operands) - far),
        out_specs=out_places or [VMEM] * len(outs),
        scratch_shapes=scratch,
        cost_estimate=pl.CostEstimate(flops=int(cost * 1e9), bytes_accessed=int(cost * 1e6), transcendentals=0),
        compiler_params=pltpu.CompilerParams(vmem_limit_bytes=32 << 20),
    )(*held, *operands[far:])


def shape(dims, dtype):
    return jax.ShapeDtypeStruct(dims, dtype)


def padded(rows):
    return -(-rows // SUBLANES) * SUBLANES


def split3(value):
    high = value.astype(BF16)
    rest = value - high.astype(F32)
    mid = rest.astype(BF16)
    return high, mid, (rest - mid.astype(F32)).astype(BF16)


def stacked(value, heads):
    parts = list(split3(value))
    fill = padded(3 * heads) - 3 * heads
    if fill:
        parts.append(jnp.zeros((fill, LANES), BF16))
    return jnp.concatenate([part.astype(F32) for part in parts], axis=0).astype(BF16)


def unstacked(rows, heads):
    rows = rows.astype(F32)
    return rows[:heads] + rows[heads : 2 * heads] + rows[2 * heads : 3 * heads]


def triangle(tokens):
    row = lax.broadcasted_iota(jnp.int32, (tokens, tokens), 0)
    col = lax.broadcasted_iota(jnp.int32, (tokens, tokens), 1)
    return row, col


def column_sums(decay):
    heads, tokens = decay.shape
    row, col = triangle(tokens)
    lower = jnp.where(row >= col, 1.0, 0.0).astype(BF16)
    sums = [
        lax.dot_general(lower, part, (((1,), (1,)), ((), ())), preferred_element_type=F32) for part in split3(decay)
    ]
    return sums[0] + (sums[1] + sums[2])


def row_sums(decay):
    row, col = triangle(decay.shape[1])
    upper = jnp.where(row <= col, 1.0, 0.0).astype(F32)
    return jnp.dot(decay, upper, precision=HIGHEST)


def odd(axis, step=0):
    return (lax.axis_index(axis) >> step) % 2 == 1


def fetch(sources, targets, semaphores):
    copies = [
        pltpu.make_async_copy(source, target, semaphores.at[index])
        for index, (source, target) in enumerate(zip(sources, targets))
    ]
    for copy in copies:
        copy.start()
    return copies


def states_kernel(keys_far, values_far, decay_far, message, keys, values, decay, tails, semaphores):
    decay_copy, *copies = fetch((decay_far, keys_far, values_far), (decay, keys, values), semaphores)
    decay_copy.wait()
    heads, tokens = decay.shape
    width = keys.shape[1] // heads
    column = column_sums(decay[...])
    tail = jnp.exp(column[tokens - 1 : tokens, :] - column)
    for head in range(heads):
        tails[:, head * width : (head + 1) * width] = jnp.broadcast_to(tail[:, head : head + 1], (tokens, width))
    total = jnp.sum(decay[...], axis=1, keepdims=True)
    message[heads * width :, :] = stacked(jnp.broadcast_to(jnp.exp(total), (heads, LANES)), heads)
    for copy in copies:
        copy.wait()
    for head in range(heads):
        own = slice(head * width, (head + 1) * width)
        faded = (values[:, own].astype(F32) * tails[:, own]).astype(BF16)
        state = lax.dot_general(
            keys[:, own], faded, (((0,), (0,)), ((), ())), preferred_element_type=F32
        )
        message[own, :] = state.astype(BF16)


def weights_kernel(far_count, split, weight_far, _, *refs):
    *weights, token, semaphores = refs
    columns = weights[0].shape[1]
    me = lax.axis_index("head")
    copies = []

    def copy(owner, first, end, target):
        start = pl.multiple_of(owner * columns + first, LANES)
        source = weight_far.at[:, pl.ds(start, end - first)]
        copies.append(pltpu.make_async_copy(source, target.at[:, first:end], semaphores.at[len(copies)]))
        copies[-1].start()

    for index, target in enumerate(weights):
        far = far_count - 1 - index // 2
        owner = me ^ (far << 1) ^ (1 - index % 2)
        if far % 2:
            copy(owner, 0, split, target)
            copy(owner ^ 1, split, columns, target)
        else:
            copy(owner, 0, columns, target)
    token[...] = jnp.zeros_like(token)
    for one in copies:
        one.wait()


def within_kernel(step, query_far, keys_far, values_far, decay_far, before, before_decay, *refs):
    within, factor, query, keys, values, decay, semaphores = refs
    for copy in fetch((query_far, keys_far, values_far, decay_far), (query, keys, values, decay), semaphores):
        copy.wait()
    heads, tokens = decay.shape
    width = keys.shape[1] // heads
    column = column_sums(decay[...])
    line = row_sums(decay[...])
    grown = jnp.exp(column)
    scale = jnp.where(odd("ctx", step), before_decay[...], 0.0 * before_decay[...])
    row, col = triangle(tokens)
    for head in range(heads):
        own = slice(head * width, (head + 1) * width)
        scores = lax.dot_general(
            query[:, own], keys[:, own], (((1,), (1,)), ((), ())), preferred_element_type=F32
        )
        differ = jnp.where(row >= col, column[:, head : head + 1] - line[head : head + 1, :], -1e30)
        weights = (jnp.exp(differ) * scores).astype(BF16)
        carried = jnp.dot(query[:, own], before[own, :].astype(BF16), preferred_element_type=F32)
        spread = jnp.broadcast_to(grown[:, head : head + 1], (tokens, width))
        within[:, own] = jnp.dot(weights, values[:, own], preferred_element_type=F32) + spread * carried
        factor[:, own] = spread * scale[head : head + 1]


def join_kernel(step, heads, *refs):
    first = step == 0
    if first:
        mine, theirs, _, joined, entering, entering_decay = refs
    else:
        mine, theirs, before, before_decay, joined, entering, entering_decay = refs
    later = odd("ctx", step)
    rows = mine.shape[0] - padded(3 * heads)
    width = rows // heads
    my_decay = unstacked(mine[rows:, :], heads)
    their_decay = unstacked(theirs[rows:, :], heads)
    one = jnp.ones_like(my_decay)
    for_theirs = jnp.where(later, my_decay, one)
    for_mine = jnp.where(later, one, their_decay)
    if first:
        for_entering = jnp.where(later, one, 0.0 * one)
        entering_decay[...] = jnp.where(later, their_decay, one)
    else:
        for_entering = jnp.where(later, before_decay[...], 0.0 * one)
        entering_decay[...] = before_decay[...] * jnp.where(later, their_decay, one)
    for head in range(heads):
        own = slice(head * width, (head + 1) * width)
        row = slice(head, head + 1)
        received = theirs[own, :].astype(F32)
        joined[own, :] = (for_theirs[row] * received + for_mine[row] * mine[own, :].astype(F32)).astype(BF16)
        added = for_entering[row] * received
        entering[own, :] = added if first else before[own, :] + added
    if joined.shape[0] > rows:
        joined[rows:, :] = stacked(my_decay * their_decay, heads)


def attend_kernel(heads, query, within, factor, theirs, gain, message):
    tokens, full = query.shape
    width = full // heads
    squares = jnp.zeros((tokens, width), F32)
    for head in range(heads):
        own = slice(head * width, (head + 1) * width)
        carried = jnp.dot(query[:, own], theirs[own, :], preferred_element_type=F32)
        attn = within[:, own] + factor[:, own] * carried
        squares = squares + attn * attn
        message[:, own] = (attn * gain[:, own]).astype(BF16)
    message[:, full:] = squares.astype(BF16)


def squares_row(mine, theirs, full):
    column = jnp.sum(mine[:, full:].astype(F32) + theirs[:, full:].astype(F32), axis=1, keepdims=True)
    row, col = triangle(mine.shape[0])
    return jnp.sum(jnp.where(row == col, column, 0.0), axis=0, keepdims=True)


def ahead_kernel(full, mine, weight, result):
    result[...] = jnp.dot(mine[:, :full], weight[...], preferred_element_type=F32)


def away_kernel(full, first_block, leading, partial, mine, theirs, their_weight, *refs):
    *received, message = refs
    tokens = mine.shape[0]
    blocks = message.shape[0] // tokens
    columns = slice(first_block * LANES, (first_block + blocks) * LANES)
    result = partial[:, columns] + jnp.dot(theirs[:, :full], their_weight[:, columns], preferred_element_type=F32)
    for block in range(blocks):
        there = slice(block * tokens, (block + 1) * tokens)
        part = result[:, block * LANES : (block + 1) * LANES]
        for other in received:
            part = part + other[there, :].astype(F32)
        message[there, :] = part.astype(BF16)
    if leading:
        total = squares_row(mine, theirs, full)
        for other in received:
            total = total + unstacked(other[blocks * tokens :, :], 1)
        message[blocks * tokens :, :] = stacked(total, 1)


def home_kernel(full, mine, theirs, my_weight, their_weight, result):
    result[...] = jnp.dot(mine[:, :full], my_weight[...], preferred_element_type=F32) + jnp.dot(
        theirs[:, :full], their_weight[...], preferred_element_type=F32
    )


def scaled(partial, first_block, received, scale, out):
    tokens, columns = out.shape
    for block in range(columns // LANES):
        summed = partial[:, (first_block + block) * LANES : (first_block + block + 1) * LANES]
        for other in received:
            summed = summed + other[block * tokens : (block + 1) * tokens, :].astype(F32)
        out[:, block * LANES : (block + 1) * LANES] = (summed * scale).astype(BF16)


def middle_kernel(full, cuts, count, sent, partial, *refs):
    received, (scale, *outs) = refs[: len(cuts) * count], refs[len(cuts) * count :]
    groups = [received[part * count : (part + 1) * count] for part in range(len(cuts))]
    total = unstacked(sent[sent.shape[0] - SUBLANES :, :], 1)
    for other in groups[-1]:
        total = total + unstacked(other[other.shape[0] - SUBLANES :, :], 1)
    row, col = triangle(partial.shape[0])
    total = jnp.sum(jnp.where(row == col, total, 0.0), axis=1, keepdims=True)
    factor = lax.rsqrt(total / (full * lax.axis_size("head")) + 1e-05)
    scale[...] = factor
    for first_block, group, out in zip(cuts, groups, outs):
        scaled(partial, first_block, group, factor, out)


def last_kernel(first_block, done_count, partial, scale, *refs):
    done, received = refs[:done_count], refs[done_count:-3]
    out, staged, semaphores = refs[-3:]
    copies = []

    def write(source, column):
        there = out.at[:, column : column + source.shape[1]]
        copies.append(pltpu.make_async_copy(source, there, semaphores.at[len(copies)]))
        copies[-1].start()

    column = 0
    for part in done:
        write(part, column)
        column += part.shape[1]
    scaled(partial, first_block, received, scale[...], staged)
    write(staged, column)
    for copy in copies:
        copy.wait()


def local(query, keys, values, log_decay, norm_gain, out_weight):
    tokens, full = query.shape
    heads = log_decay.shape[1]
    steps = lax.axis_size("ctx").bit_length() - 1
    groups = lax.axis_size("head")
    columns = out_weight.shape[1] // groups
    decay = log_decay.T
    message_shape = shape((full + padded(3 * heads), LANES), BF16)
    dma = pltpu.SemaphoreType.DMA

    def swap(value, axis, bit):
        count = lax.axis_size(axis)
        return lax.ppermute(value, axis, [(i, i ^ bit) for i in range(count)])

    blocks = [pltpu.VMEM(array.shape, array.dtype) for array in (query, keys, values, decay)]
    (message,) = call(
        states_kernel,
        [message_shape],
        (keys, values, decay),
        far=3,
        scratch=[*blocks[1:], pltpu.VMEM((tokens, full), F32), dma((3,))],
    )
    theirs = swap(message, "ctx", 1)

    far_count = groups // 2
    blocks_out = columns // LANES
    cuts = [0, blocks_out * 5 // 12, blocks_out - blocks_out // 4, blocks_out]
    *weights, token = call(
        functools.partial(weights_kernel, far_count, cuts[-2] * LANES),
        [shape((full, columns), BF16)] * (2 * far_count) + [shape((8, LANES), F32)],
        (out_weight, message),
        far=1,
        scratch=[dma((3 * far_count,))],
        cost=2.0,
    )
    my_weights, their_weights = {}, {}
    for index in range(0, 2 * far_count, 2):
        far = far_count - 1 - index // 2
        their_weights[far] = swap(weights[index], "head", 1)
        my_weights[far] = weights[index + 1]

    entering = (token,)
    for step in range(steps - 1):
        message, *entering = call(
            functools.partial(join_kernel, step, heads),
            [
                message_shape if step < steps - 2 else shape((full, LANES), BF16),
                shape((full, LANES), F32),
                shape((heads, LANES), F32),
            ],
            (message, theirs, *entering),
            cost=30.0 if step == steps - 2 else 0.1,
        )
        theirs = swap(message, "ctx", 2 << step)
    within, factor = call(
        functools.partial(within_kernel, steps - 1),
        [shape((tokens, full), F32)] * 2,
        (query, keys, values, decay, *entering),
        far=4,
        scratch=[*blocks, dma((4,))],
        cost=1.0,
    )
    (mine,) = call(
        functools.partial(attend_kernel, heads),
        [shape((tokens, full + LANES), BF16)],
        (query, within, factor, theirs, norm_gain[None, :]),
    )
    mate = swap(mine, "head", 1)
    ahead = {}
    for far in range(1, far_count):
        (ahead[far],) = call(
            functools.partial(ahead_kernel, full),
            [shape((tokens, columns), F32)],
            (mine, my_weights[far]),
            cost=0.4,
        )

    received = [[[] for _ in range(PARTS)] for _ in range(far_count)]
    reach = far_count // 2
    sent = None
    while reach:
        for far in range(reach, 2 * reach):
            for part, (first, end) in enumerate(zip(cuts[:-1], cuts[1:])):
                (away,) = call(
                    functools.partial(away_kernel, full, first, part == PARTS - 2),
                    [shape(((end - first) * tokens + SUBLANES * (part == PARTS - 2), LANES), BF16)],
                    (ahead[far], mine, mate, their_weights[far], *received[far][part]),
                    cost=0.2,
                )
                if part == PARTS - 2 and sent is None:
                    sent = away
                hop = 3 if reach == 1 and part == PARTS - 1 else reach << 1
                received[far - reach][part].append(swap(away, "head", hop))
        reach //= 2
    (partial,) = call(
        functools.partial(home_kernel, full),
        [shape((tokens, columns), F32)],
        (mine, mate, my_weights[0], their_weights[0]),
        cost=0.6,
    )
    widths = [(end - first) * LANES for first, end in zip(cuts[:-1], cuts[1:])]
    scale, *done = call(
        functools.partial(middle_kernel, full, cuts[: PARTS - 1], len(received[0][0])),
        [shape((tokens, 1), F32)] + [shape((tokens, width), BF16) for width in widths[:-1]],
        (sent, partial, *(other for group in received[0][:-1] for other in group)),
        cost=0.3,
    )
    (mixed,) = call(
        functools.partial(last_kernel, cuts[PARTS - 1], len(done)),
        [shape((tokens, columns), BF16)],
        (partial, scale, *done, *received[0][PARTS - 1]),
        out_places=[FAR],
        scratch=[pltpu.VMEM((tokens, widths[-1]), BF16), dma((PARTS,))],
    )
    return mixed


def solution(mesh):
    placed = (
        P("ctx", "head"),
        P("ctx", "head"),
        P("ctx", "head"),
        P("ctx", "head"),
        P("head"),
        P("head", None),
    )
    return jax.shard_map(
        local, mesh=mesh, in_specs=placed, out_specs=P("ctx", "head"), check_vma=False
    )
```
